32 devices in a mesh: dev: 32 (over z, y, x, core).
Axes of the slice: x: 2, y: 2, z: 4, core: 2. Of those that a mesh axis runs over, the one named last changes fastest.
Arguments:
- tokens: bfloat16 [16384, 1024], P('dev'), may hold values from -6 to 6
- cotangent: bfloat16 [16384, 1024], P('dev'), may hold values from -6 to 6
- segment_ids: int32 [16384], P('dev'), may hold values from 0 to 14, never falling along the last dimension, each value on 1 to 1370 neighbouring positions
- validity: int32 [16384], P('dev'), may hold values 0 or 1
- first_gain: bfloat16 [1024], P('dev'), may hold values from 0.099609375 to 1.8984375
- first_bias: bfloat16 [1024], P('dev'), may hold values from -4 to 4
- query_weight: bfloat16 [1024, 1024], P('dev'), may hold values from -0.25 to 0.25
- query_bias: bfloat16 [1024], P('dev'), may hold values from -4 to 4
- key_weight: bfloat16 [1024, 1024], P('dev'), may hold values from -0.25 to 0.25
- value_weight: bfloat16 [1024, 1024], P('dev'), may hold values from -0.1875 to 0.1875
- value_bias: bfloat16 [1024], P('dev'), may hold values from -4 to 4
- output_weight: bfloat16 [1024, 1024], P('dev'), may hold values from -0.75 to 0.75
- output_bias: bfloat16 [1024], P('dev'), may hold values from -4 to 4
- attention_scale: bfloat16 [1024], P('dev'), may hold values from 0.5 to 2
- second_gain: bfloat16 [1024], P('dev'), may hold values from 0.099609375 to 1.8984375
- second_bias: bfloat16 [1024], P('dev'), may hold values from -4 to 4
- hidden_weight: bfloat16 [1024, 4096], P('dev'), may hold values from -0.1875 to 0.1875
- hidden_bias: bfloat16 [4096], P('dev'), may hold values from -4 to 4
- project_weight: bfloat16 [4096, 1024], P('dev'), may hold values from -0.09375 to 0.09375
- project_bias: bfloat16 [1024], P('dev'), may hold values from -4 to 4
- dense_scale: bfloat16 [1024], P('dev'), may hold values from 0.5 to 2
Outputs:
- layer_output: bfloat16 [16384, 1024], P('dev')
- input_gradient: float32 [16384, 1024], P('dev')
- first_gain_grad: float32 [1024], P('dev')
- first_bias_grad: float32 [1024], P('dev')
- query_weight_grad: float32 [1024, 1024], P('dev')
- query_bias_grad: float32 [1024], P('dev')
- key_weight_grad: float32 [1024, 1024], P('dev')
- value_weight_grad: float32 [1024, 1024], P('dev')
- value_bias_grad: float32 [1024], P('dev')
- output_weight_grad: float32 [1024, 1024], P('dev')
- output_bias_grad: float32 [1024], P('dev')
- attention_scale_grad: float32 [1024], P('dev')
- second_gain_grad: float32 [1024], P('dev')
- second_bias_grad: float32 [1024], P('dev')
- hidden_weight_grad: float32 [1024, 4096], P('dev')
- hidden_bias_grad: float32 [4096], P('dev')
- project_weight_grad: float32 [4096, 1024], P('dev')
- project_bias_grad: float32 [1024], P('dev')
- dense_scale_grad: float32 [1024], P('dev')
The draws below stay inside these ranges and needn't reach their ends.
Inputs may be any that keep to these rules, and one draw needn't show every extreme that they name: `segment_ids`: never falls along the rows; each of the 15 images takes 1 to 1370 consecutive rows, and one takes exactly 1370.
All inputs are finite; a program needn't handle non-finite values. No bound on the sum of `validity` on one device may be relied on, other than what follows from the above.
Results may differ from the reference program's by a relative error of at most 0.013.
The reference program's roundings to bfloat16 on the way count: a program that leaves them out, or rounds other values in their place, can miss the bound.
Values may be sent and summed in bfloat16 or wider, within the bound.
No kernel may reach another device: no remote copies, remote signals or barrier semaphores. Data moves between devices by JAX's collectives and lax.ppermute only.
A program may use at most 192 MiB of HBM per device.

```python
import math
from functools import partial
import jax
import jax.numpy as jnp
import numpy as np
from jax import lax

D = 1024
HEADS = 16
HEAD_DIM = 64
FF = 4096
IMG = 1370
TOK_DEV = 512
TOKENS = 16384
IMAGES = 15
REACH = 3


def touch_ends(values, rng, low, high):
    spot = [jax.random.randint(jax.random.fold_in(rng, axis), (), 0, length) for axis, length in enumerate(values.shape)]
    main_axis = values.shape.index(max(values.shape))
    beside = spot[:main_axis] + [(spot[main_axis] + 1) % values.shape[main_axis]] + spot[main_axis + 1:]
    return values.at[tuple(spot)].set(low).at[tuple(beside)].set(high)


def raised(drawn, rng, source, target, blocks, factor):
    def block_of(axis_at):
        return (jnp.arange(drawn.shape[axis_at]) // (drawn.shape[axis_at] // blocks)).reshape((-1,) + (1,) * (drawn.ndim - 1 - axis_at))

    near = jax.random.permutation(rng, blocks)[block_of(target)]
    other_side = (block_of(target) + blocks // 2) % blocks
    return jnp.where((block_of(source) == near) | (block_of(source) == other_side), factor * drawn, drawn)


def block_levels(key, shape, shards, least, top_value):
    def one(position, parts):
        draws = jax.random.uniform(jax.random.fold_in(jax.random.fold_in(key, 6), position), (parts,), jnp.float32, least / len(shards), top_value / len(shards))
        return jnp.repeat(jnp.exp(draws), shape[position] // parts).reshape((-1,) + (1,) * (len(shape) - position - 1))

    level = one(*shards[0])
    for cut in shards[1:]:
        level = level * one(*cut)
    return level


def split_up(count, total, reach, slope):
    portions = [(1 << 20) // math.isqrt(standing ** slope) + 1 for standing in range(2, count + 1)]
    surplus, given = total - reach - (count - 1), [1] * (count - 1)
    while surplus > 0:
        candidates = [i for i in range(count - 1) if given[i] < reach]
        mass, remaining = sum([portions[i] for i in candidates]), surplus
        for i in candidates:
            addition = min(reach - given[i], max(1, remaining * portions[i] // mass), surplus)
            given[i] = given[i] + addition
            surplus = surplus - addition
    return np.array([reach] + given)


def uneven(rng, count, total, bound, slope):
    if count == 2:
        one = jax.random.randint(rng, (), max(1, total - bound), min(bound, total - 1) + 1)
        return jnp.stack([one, total - one])
    sizes = jnp.asarray(split_up(count, total, bound, slope), jnp.int32)
    pairs = (count - 1) // 2
    giver, sink = sizes[1:1 + 2 * pairs:2], sizes[2:2 + 2 * pairs:2]
    room = jnp.minimum(giver - 1, bound - sink)
    passed = jax.random.randint(jax.random.fold_in(rng, 1), (pairs,), 0, 1 << 20) % (room + 1)
    sizes = sizes.at[1:1 + 2 * pairs:2].set(giver - passed).at[2:2 + 2 * pairs:2].set(sink + passed)
    return sizes[jax.random.permutation(jax.random.fold_in(rng, 2), count)]


def normal_values(stream_key, extent, deviation, bound, pieces=(), kind=jnp.bfloat16):
    array = deviation * jax.random.normal(stream_key, extent, jnp.float32)
    if pieces:
        array = array * block_levels(stream_key, extent, pieces, -0.22, 0.18)
    return jnp.clip(array, -bound, bound).astype(kind)


def gaussian_with(rng, dims, scale, reach, pieces, heavy, held_as=jnp.bfloat16):
    array = scale * jax.random.normal(rng, dims, jnp.float32)
    if pieces:
        array = array * block_levels(rng, dims, pieces, -0.22, 0.18)
    return jnp.clip(raised(array, jax.random.fold_in(rng, 3), *heavy), -reach, reach).astype(held_as)


def setup_inputs(seed: int = 0) -> dict:
    seeds = jax.random.split(jax.random.key(seed), 22)
    tokens = normal_values(seeds[0], (TOKENS, D), 1.0, 6.0, ((0, 32),))
    cotangent = gaussian_with(seeds[1], (TOKENS, D), 1.0, 6.0, ((0, 32),), (0, 1, 32, 2.75))
    segment_ids = jnp.searchsorted(jnp.cumsum(uneven(seeds[2], IMAGES, TOKENS, IMG, 0)), jnp.arange(TOKENS), side="right").astype(jnp.int32)
    validity = touch_ends((jax.random.randint(seeds[3], (TOKENS,), 0, 8) < 7).astype(jnp.int32), jax.random.fold_in(seeds[3], 1), 0, 1)
    first_gain = jnp.clip(1.0 + 0.18 * jax.random.normal(seeds[4], (D,), jnp.float32), 0.099609375, 1.8984375).astype(jnp.bfloat16)
    first_bias = normal_values(seeds[5], (D,), 0.3, 4.0, ((0, 32),))
    query_weight = normal_values(seeds[6], (D, D), (D // 2) ** -0.5, 0.25, ((0, 32),))
    query_bias = normal_values(seeds[7], (D,), 0.5, 4.0, ((0, 32),))
    key_weight = normal_values(seeds[8], (D, D), (D // 2) ** -0.5, 0.25, ((0, 32),))
    value_weight = normal_values(seeds[9], (D, D), D ** -0.5, 0.1875, ((0, 32),))
    value_bias = normal_values(seeds[10], (D,), 0.5, 4.0, ((0, 32),))
    output_weight = normal_values(seeds[11], (D, D), (D // 16) ** -0.5, 0.75, ((0, 32),))
    output_bias = normal_values(seeds[12], (D,), 0.5, 4.0, ((0, 32),))
    attention_scale = jnp.clip(jnp.exp(math.log(2.0) - 1.3862944 * jax.random.uniform(seeds[13], (D,), jnp.float32) ** block_levels(seeds[13], (D,), ((0, 32),), -0.2, 0.2)), 0.5, 2.0).astype(jnp.bfloat16)
    second_gain = jnp.clip(1.0 + 0.18 * jax.random.normal(seeds[14], (D,), jnp.float32), 0.099609375, 1.8984375).astype(jnp.bfloat16)
    second_bias = normal_values(seeds[15], (D,), 0.3, 4.0, ((0, 32),))
    hidden_weight = normal_values(seeds[16], (D, FF), D ** -0.5, 0.1875, ((0, 32),))
    hidden_bias = normal_values(seeds[17], (FF,), 0.5, 4.0, ((0, 32),))
    project_weight = normal_values(seeds[18], (FF, D), FF ** -0.5, 0.09375, ((0, 32),))
    project_bias = normal_values(seeds[19], (D,), 0.5, 4.0, ((0, 32),))
    dense_scale = jnp.clip(jnp.exp(math.log(2.0) - 1.3862944 * jax.random.uniform(seeds[20], (D,), jnp.float32) ** block_levels(seeds[20], (D,), ((0, 32),), -0.2, 0.2)), 0.5, 2.0).astype(jnp.bfloat16)
    return dict(tokens=tokens, cotangent=cotangent, segment_ids=segment_ids, validity=validity, first_gain=first_gain, first_bias=first_bias, query_weight=query_weight, query_bias=query_bias, key_weight=key_weight, value_weight=value_weight, value_bias=value_bias, output_weight=output_weight, output_bias=output_bias, attention_scale=attention_scale, second_gain=second_gain, second_bias=second_bias, hidden_weight=hidden_weight, hidden_bias=hidden_bias, project_weight=project_weight, project_bias=project_bias, dense_scale=dense_scale)


@jax.custom_vjp
def low(v):
    return lax.optimization_barrier(v.astype(jnp.bfloat16)).astype(jnp.float32)

@jax.custom_vjp
def low_back(v):
    return v

def low_keep(v):
    return (low(v), None)

def low_pass(kept, grad):
    return (grad,)

def back_keep(v):
    return (v, None)

def back_low(kept, grad):
    return (low(grad),)
low.defvjp(low_keep, low_pass)
low_back.defvjp(back_keep, back_low)
norm_eps = 1e-06

def dot_highest(left_rows, right_rows):
    return jnp.dot(left_rows, right_rows, precision=lax.Precision.HIGHEST, preferred_element_type=jnp.float32)

def layer_norm(row_values, gain_row, bias_row):
    center = row_values - lax.optimization_barrier(jnp.mean(row_values, axis=-1, keepdims=True))
    spread = lax.optimization_barrier(jnp.mean(center * center, axis=-1, keepdims=True))
    return center * lax.rsqrt(spread + norm_eps) * gain_row + bias_row

def whole_layer(labels, inputs, first_gain, first_bias, query_weight, query_bias, key_weight, value_weight, value_bias, output_weight, output_bias, attention_scale, second_gain, second_bias, hidden_weight, hidden_bias, project_weight, project_bias, dense_scale):
    query_label, key_label = labels
    normed = low(layer_norm(inputs, first_gain, first_bias))
    queries = low_back(low(dot_highest(normed, query_weight) + query_bias))
    key_rows = low_back(low(dot_highest(normed, key_weight)))
    value_rows = low_back(low(dot_highest(normed, value_weight) + value_bias))
    margin = REACH * TOK_DEV
    window_width = (2 * REACH + 1) * TOK_DEV
    padded_keys = jnp.pad(key_rows, ((margin, margin), (0, 0)))
    padded_values = jnp.pad(value_rows, ((margin, margin), (0, 0)))
    padded_labels = jnp.pad(key_label, (margin, margin))
    row_index = lax.broadcasted_iota(jnp.int32, (TOK_DEV, window_width), 0)
    col_index = lax.broadcasted_iota(jnp.int32, (TOK_DEV, window_width), 1)
    diagonal = col_index == row_index + margin

    def attend_block(block_index):
        row_start = (block_index * TOK_DEV).astype(jnp.int32)
        query_block = lax.dynamic_slice_in_dim(queries, row_start, TOK_DEV, 0).reshape(TOK_DEV, HEADS, HEAD_DIM)
        key_block = lax.dynamic_slice_in_dim(padded_keys, row_start, window_width, 0).reshape(window_width, HEADS, HEAD_DIM)
        value_block = lax.dynamic_slice_in_dim(padded_values, row_start, window_width, 0).reshape(window_width, HEADS, HEAD_DIM)
        query_tags = lax.dynamic_slice_in_dim(query_label, row_start, TOK_DEV, 0)
        key_tags = lax.dynamic_slice_in_dim(padded_labels, row_start, window_width, 0)
        allowed = (query_tags[:, None] == key_tags[None, :]) | diagonal
        scores = jnp.einsum('qhd,khd->hqk', query_block, key_block, precision=lax.Precision.HIGHEST) * HEAD_DIM ** (-0.5)
        scores = low_back(jnp.where(allowed[None], scores, -1e+30))
        row_peak = lax.optimization_barrier(jnp.max(scores, axis=-1, keepdims=True))
        exponent = jnp.exp(scores - row_peak)
        weights = exponent / lax.optimization_barrier(jnp.sum(exponent, axis=-1, keepdims=True))
        outputs = jnp.einsum('hqk,khd->qhd', low(weights), value_block, precision=lax.Precision.HIGHEST)
        return outputs.reshape(TOK_DEV, D)
    attended = lax.map(jax.checkpoint(attend_block), jnp.arange(TOKENS // TOK_DEV, dtype=jnp.int32))
    attended = low_back(low(attended.reshape(TOKENS, D)))
    branch = low_back(dot_highest(attended, output_weight) + output_bias)
    middle = inputs + attention_scale * branch
    normed_two = low(layer_norm(middle, second_gain, second_bias))
    hidden = low_back(dot_highest(normed_two, hidden_weight) + hidden_bias)
    active = low(jax.nn.gelu(hidden, approximate=False))
    dense_out = low_back(dot_highest(active, project_weight) + project_bias)
    return middle + dense_scale * dense_out

def reference(tokens, cotangent, segment_ids, validity, first_gain, first_bias, query_weight, query_bias, key_weight, value_weight, value_bias, output_weight, output_bias, attention_scale, second_gain, second_bias, hidden_weight, hidden_bias, project_weight, project_bias, dense_scale):
    query_label = (segment_ids + 1).astype(jnp.int32)
    key_label = jnp.where(validity == 1, segment_ids + 1, 0).astype(jnp.int32)
    floats = (tokens.astype(jnp.float32), first_gain.astype(jnp.float32), first_bias.astype(jnp.float32), query_weight.astype(jnp.float32), query_bias.astype(jnp.float32), key_weight.astype(jnp.float32), value_weight.astype(jnp.float32), value_bias.astype(jnp.float32), output_weight.astype(jnp.float32), output_bias.astype(jnp.float32), attention_scale.astype(jnp.float32), second_gain.astype(jnp.float32), second_bias.astype(jnp.float32), hidden_weight.astype(jnp.float32), hidden_bias.astype(jnp.float32), project_weight.astype(jnp.float32), project_bias.astype(jnp.float32), dense_scale.astype(jnp.float32))
    result, pullback = jax.vjp(partial(whole_layer, (query_label, key_label)), *floats)
    input_gradient, first_gain_grad, first_bias_grad, query_weight_grad, query_bias_grad, key_weight_grad, value_weight_grad, value_bias_grad, output_weight_grad, output_bias_grad, attention_scale_grad, second_gain_grad, second_bias_grad, hidden_weight_grad, hidden_bias_grad, project_weight_grad, project_bias_grad, dense_scale_grad = pullback(cotangent.astype(jnp.float32))
    return (result.astype(jnp.bfloat16), input_gradient, first_gain_grad, first_bias_grad, query_weight_grad, query_bias_grad, key_weight_grad, value_weight_grad, value_bias_grad, output_weight_grad, output_bias_grad, attention_scale_grad, second_gain_grad, second_bias_grad, hidden_weight_grad, hidden_bias_grad, project_weight_grad, project_bias_grad, dense_scale_grad)
```

```python
from functools import partial
import jax
import jax.numpy as jnp
from jax import lax
from jax.experimental import pallas as pl
from jax.experimental.pallas import tpu as pltpu
from jax.sharding import PartitionSpec as P

HEAD_DIM = 64
PAIR = 2 * HEAD_DIM
IMG = 1370
BLK = 256
norm_eps = 1e-06
bf16 = jnp.bfloat16
f32 = jnp.float32
NEG = -1e30


def layer_norm(row_values, gain_row, bias_row):
    center = row_values - jnp.mean(row_values, axis=-1, keepdims=True)
    spread = jnp.mean(center * center, axis=-1, keepdims=True)
    return center * lax.rsqrt(spread + norm_eps) * gain_row + bias_row


def gelu_exact(arguments):
    return jax.nn.gelu(arguments, approximate=False)


def product(a, b):
    return jnp.dot(a, b, preferred_element_type=f32)


def inner_rows(a, b):
    return lax.dot_general(a, b, (((0,), (0,)), ((), ())), preferred_element_type=f32)


def against(a, b):
    return lax.dot_general(a, b, (((1,), (1,)), ((), ())), preferred_element_type=f32)


def column_sums(rows):
    return jnp.sum(rows.astype(f32), axis=0)


def head_lanes(h):
    lane = lax.broadcasted_iota(jnp.int32, (1, PAIR), 1)
    return (lane >= h * HEAD_DIM) & (lane < (h + 1) * HEAD_DIM)


def own_head(block, h):
    return jnp.where(head_lanes(h), block, jnp.zeros_like(block))


def offsets():
    shape = (BLK, BLK)
    return lax.broadcasted_iota(jnp.int32, shape, 1) - lax.broadcasted_iota(jnp.int32, shape, 0)


def attend_kernel(first, lo, hi, q_ref, k_ref, v_ref, ql_ref, kl_ref, o_ref, lse_ref, s_ref, m_ref, l_ref, a_ref):
    block = pl.program_id(1)
    start, stop = lo[block], hi[block]
    apart = offsets()
    ql = ql_ref[...]
    heads = [own_head(q_ref[...], h) for h in range(2)]
    m_ref[...] = jnp.full(m_ref.shape, NEG, f32)
    l_ref[...] = jnp.zeros(l_ref.shape, f32)
    a_ref[...] = jnp.zeros(a_ref.shape, f32)

    def scores(kb, _):
        rows = pl.ds(pl.multiple_of(kb * BLK, BLK), BLK)
        k = k_ref[rows, :]
        seen = (ql == kl_ref[:, rows]) | (apart == (first + block - kb) * BLK)
        for h in range(2):
            s = jnp.where(seen, against(heads[h], k), NEG)
            s_ref[h, kb] = s
            m_ref[h] = jnp.maximum(m_ref[h], jnp.maximum(s[:, :128], s[:, 128:]))
        return 0

    lax.fori_loop(start, stop, scores, 0)
    peaks = [jnp.max(m_ref[h], axis=1, keepdims=True) for h in range(2)]

    def values(kb, _):
        rows = pl.ds(pl.multiple_of(kb * BLK, BLK), BLK)
        v = v_ref[rows, :]
        for h in range(2):
            p = jnp.exp(s_ref[h, kb] - peaks[h])
            l_ref[h] = l_ref[h] + (p[:, :128] + p[:, 128:])
            a_ref[h] = a_ref[h] + product(p.astype(bf16), v)
        return 0

    lax.fori_loop(start, stop, values, 0)
    totals = [jnp.sum(l_ref[h], axis=1, keepdims=True) for h in range(2)]
    first_head = head_lanes(0)
    o_ref[...] = jnp.where(first_head, a_ref[0] / totals[0], a_ref[1] / totals[1])
    lse_ref[...] = jnp.where(first_head, peaks[0] + jnp.log(totals[0]), peaks[1] + jnp.log(totals[1]))


def query_kernel(first, lo, hi, q_ref, k_ref, v_ref, ql_ref, kl_ref, do_ref, lse_ref, dl_ref, dq_ref, a_ref):
    block = pl.program_id(1)
    apart = offsets()
    ql = ql_ref[...]
    q = [own_head(q_ref[...], h) for h in range(2)]
    do = [own_head(do_ref[...], h) for h in range(2)]
    lse = [lse_ref[:, h * HEAD_DIM : h * HEAD_DIM + 1] for h in range(2)]
    delta = [dl_ref[:, h * HEAD_DIM : h * HEAD_DIM + 1] for h in range(2)]
    a_ref[...] = jnp.zeros(a_ref.shape, f32)

    def step(kb, _):
        rows = pl.ds(pl.multiple_of(kb * BLK, BLK), BLK)
        k = k_ref[rows, :]
        v = v_ref[rows, :]
        seen = (ql == kl_ref[:, rows]) | (apart == (first + block - kb) * BLK)
        for h in range(2):
            p = jnp.exp(jnp.where(seen, against(q[h], k), NEG) - lse[h])
            ds = (p * (against(do[h], v) - delta[h])).astype(bf16)
            a_ref[h] = a_ref[h] + product(ds, k)
        return 0

    lax.fori_loop(lo[block], hi[block], step, 0)
    dq_ref[...] = (jnp.where(head_lanes(0), a_ref[0], a_ref[1]) * (HEAD_DIM**-0.5)).astype(bf16)


def key_kernel(first, lo, hi, q_ref, k_ref, v_ref, ql_ref, kl_ref, do_ref, st_ref, dk_ref, dv_ref, a_ref, b_ref):
    block = pl.program_id(1)
    pair = pl.program_id(0)
    apart = offsets()
    kl = kl_ref[...]
    k = [own_head(k_ref[...], h) for h in range(2)]
    v = [own_head(v_ref[...], h) for h in range(2)]
    a_ref[...] = jnp.zeros(a_ref.shape, f32)
    b_ref[...] = jnp.zeros(b_ref.shape, f32)

    def step(qb, _):
        rows = pl.ds(pl.multiple_of(qb * BLK, BLK), BLK)
        q = q_ref[rows, :]
        do = do_ref[rows, :]
        seen = (kl == ql_ref[:, rows]) | (apart == (first + block - qb) * BLK)
        for h in range(2):
            lse = st_ref[0, h : h + 1, rows]
            delta = st_ref[0, 2 + h : 3 + h, rows]
            p = jnp.exp(jnp.where(seen, against(k[h], q), NEG) - lse)
            ds = (p * (against(v[h], do) - delta)).astype(bf16)
            a_ref[h] = a_ref[h] + product(ds, q)
            b_ref[h] = b_ref[h] + product(p.astype(bf16), do)
        return 0

    lax.fori_loop(lo[block], hi[block], step, 0)
    dk_ref[...] = jnp.where(head_lanes(0), a_ref[0], a_ref[1]).astype(bf16)
    dv_ref[...] = jnp.where(head_lanes(0), b_ref[0], b_ref[1]).astype(bf16)


def attention_call(kernel, grid, in_specs, out_specs, out_shape, scratch, flops):
    return pl.pallas_call(
        kernel,
        grid_spec=pltpu.PrefetchScalarGridSpec(
            num_scalar_prefetch=2,
            grid=grid,
            in_specs=in_specs,
            out_specs=out_specs,
            scratch_shapes=scratch,
        ),
        out_shape=out_shape,
        compiler_params=pltpu.CompilerParams(vmem_limit_bytes=48 * 1024 * 1024),
        cost_estimate=pl.CostEstimate(flops=flops, bytes_accessed=20_000_000, transcendentals=12_000_000),
    )


def own_bit(bit):
    return (lax.axis_index("dev") >> bit) & 1


def swap(block, bit):
    count = lax.axis_size("dev")
    return lax.ppermute(block, "dev", [(i, i ^ (1 << bit)) for i in range(count)])


def shifted(block, distance):
    count = lax.axis_size("dev")
    return lax.ppermute(block, "dev", [(i, i + distance) for i in range(count) if 0 <= i + distance < count])


def pick(block, axis, index):
    return lax.dynamic_index_in_dim(block, index, axis, keepdims=False)


def scatter_sum(block, bits, order, kind=bf16):
    bits = list(bits)
    for bit in order:
        axis = bits.index(bit)
        mine = own_bit(bit)
        sent = pick(block, axis, 1 - mine).astype(kind)
        kept = pick(block, axis, mine)
        block = kept.astype(f32) + swap(sent, bit).astype(f32)
        if kind == bf16:
            block = block.astype(bf16)
        bits.remove(bit)
    return block


def bit_view(block, count, lead):
    depth = count.bit_length() - 1
    return block.reshape((2,) * depth + (lead,) + block.shape[1:])


def on_device(
    tokens,
    cotangent,
    segment_ids,
    validity,
    first_gain,
    first_bias,
    query_weight,
    query_bias,
    key_weight,
    value_weight,
    value_bias,
    output_weight,
    output_bias,
    attention_scale,
    second_gain,
    second_bias,
    hidden_weight,
    hidden_bias,
    project_weight,
    project_bias,
    dense_scale,
):
    count = lax.axis_size("dev")
    depth = count.bit_length() - 1
    rows, width = tokens.shape
    half = width // 2
    window = 8 * rows
    assert 1 << depth == count and 2 * rows + rows >= IMG - 1 and rows % BLK == 0
    core = own_bit(0)
    shard = query_weight.shape[0]
    ff = hidden_weight.shape[1]
    parts = ff // width

    vectors = jnp.concatenate(
        [
            v.reshape(-1, shard).T
            for v in (
                first_gain,
                first_bias,
                query_bias,
                value_bias,
                output_bias,
                attention_scale,
                second_gain,
                second_bias,
                project_bias,
                dense_scale,
                hidden_bias,
            )
        ],
        axis=1,
    )
    vectors = jnp.pad(vectors, ((0, 0), (0, 128 - vectors.shape[1])))
    attention_pack = jnp.concatenate(
        [w[:, c * half : (c + 1) * half] for c in range(2) for w in (query_weight, key_weight, value_weight)]
        + [output_weight, vectors],
        axis=1,
    )
    dense_pack = jnp.concatenate(
        [hidden_weight[:, j * width : (j + 1) * width] for j in range(parts)] + [project_weight], axis=0
    )
    attention_full = lax.all_gather(attention_pack, "dev", axis=0, tiled=True)
    dense_full = lax.all_gather(dense_pack, "dev", axis=0, tiled=True).reshape(count, -1, width)

    labels = segment_ids + 1
    tag_rows = jnp.stack(
        [jnp.concatenate([labels % 256, labels // 256]), jnp.concatenate([validity, jnp.zeros_like(validity)])]
    ).astype(bf16)
    tag_rows = jnp.pad(tag_rows, ((0, 14), (0, 0)))
    own = jnp.concatenate([tokens, tag_rows])
    below = shifted(own, 2)
    above = shifted(own, -2)
    far = lax.ppermute(
        own,
        "dev",
        [(i, i - 4) for i in range(4, count, 2)] + [(i, i + 4) for i in range(1, count - 4, 2)],
    )
    mine = jnp.stack([below, own, above, far])
    theirs = swap(mine, 0)
    zero, one = jnp.where(core == 0, mine, theirs), jnp.where(core == 0, theirs, mine)
    blocks = [one[3], zero[0], one[0], zero[1], one[1], zero[2], one[2], zero[3]]
    window_tokens = jnp.concatenate([b[:rows] for b in blocks])
    tags = jnp.stack([b[rows : rows + 2] for b in blocks]).astype(jnp.int32)
    window_labels = (tags[:, 0, :rows] + 256 * tags[:, 0, rows:]).reshape(window)
    window_valid = tags[:, 1, :rows].reshape(window)
    key_label = jnp.where(window_valid == 1, window_labels, 0)
    query_label = jnp.where(window_labels == 0, -1, window_labels)
    first_row, last_row = 3 * rows, 5 * rows
    own_blocks = 2 * rows // BLK
    index = lax.broadcasted_iota(jnp.int32, (own_blocks, window), 1)
    block_labels = window_labels[first_row:last_row].reshape(own_blocks, BLK)
    lo = jnp.min(jnp.where(window_labels[None] == block_labels[:, :1], index, window), axis=1) // BLK
    hi = jnp.max(jnp.where(window_labels[None] == block_labels[:, -1:], index, -1), axis=1) // BLK + 1

    columns = attention_full[:, 4 * width :].T.astype(f32)
    (
        gain_first,
        bias_first,
        bias_query,
        bias_value,
        bias_output,
        scale_first,
        gain_second,
        bias_second,
        bias_project,
        scale_second,
    ) = [columns[i] for i in range(10)]
    bias_hidden = columns[10 : 10 + parts].reshape(parts, count, shard).transpose(1, 0, 2).reshape(ff)
    weight_qkv = lax.dynamic_slice_in_dim(attention_full, core * 3 * half, 3 * half, 1)
    weight_output = attention_full[:, 3 * width : 4 * width]

    normed_window = layer_norm(window_tokens.astype(f32), gain_first, bias_first).astype(bf16)
    start = core * half
    bias_qkv = jnp.concatenate(
        [
            lax.dynamic_slice_in_dim(bias_query, start, half),
            jnp.zeros((half,), f32),
            lax.dynamic_slice_in_dim(bias_value, start, half),
        ]
    )
    scale_qkv = jnp.concatenate([jnp.full((half,), HEAD_DIM**-0.5, f32), jnp.ones((2 * half,), f32)])
    projected = ((product(normed_window, weight_qkv) + bias_qkv) * scale_qkv).astype(bf16)

    pairs = half // PAIR
    grid = (pairs, own_blocks)
    first = first_row // BLK
    q_own = pl.BlockSpec((BLK, PAIR), lambda h, b, lo, hi: (first + b, h))
    k_own = pl.BlockSpec((BLK, PAIR), lambda h, b, lo, hi: (first + b, pairs + h))
    v_own = pl.BlockSpec((BLK, PAIR), lambda h, b, lo, hi: (first + b, 2 * pairs + h))
    q_all = pl.BlockSpec((window, PAIR), lambda h, b, lo, hi: (0, h))
    k_all = pl.BlockSpec((window, PAIR), lambda h, b, lo, hi: (0, pairs + h))
    v_all = pl.BlockSpec((window, PAIR), lambda h, b, lo, hi: (0, 2 * pairs + h))
    row_block = pl.BlockSpec((BLK, PAIR), lambda h, b, lo, hi: (b, h))
    label_rows = pl.BlockSpec((BLK, 1), lambda h, b, lo, hi: (first + b, 0))
    label_all = pl.BlockSpec((1, window), lambda h, b, lo, hi: (0, 0))
    share = 2 * rows * 1400 * half * 2
    attended_f, lse = attention_call(
        partial(attend_kernel, first),
        grid,
        [q_own, k_all, v_all, label_rows, label_all],
        [row_block, row_block],
        [jax.ShapeDtypeStruct((2 * rows, half), f32)] * 2,
        [
            pltpu.VMEM((2, window // BLK, BLK, BLK), f32),
            pltpu.VMEM((2, BLK, 128), f32),
            pltpu.VMEM((2, BLK, 128), f32),
            pltpu.VMEM((2, BLK, PAIR), f32),
        ],
        2 * share,
    )(lo, hi, projected, projected, projected, query_label[:, None], key_label[None])

    def columns_of(c, mine, theirs):
        return jnp.where(c == 0, jnp.concatenate([mine, theirs], 1), jnp.concatenate([theirs, mine], 1))

    attended_half = attended_f.astype(bf16)
    attended_low = columns_of(
        core,
        lax.dynamic_slice_in_dim(attended_half, core * rows, rows, 0),
        swap(lax.dynamic_slice_in_dim(attended_half, (1 - core) * rows, rows, 0), 0),
    )
    inputs = tokens.astype(f32)
    branch = product(attended_low, weight_output) + bias_output
    middle = inputs + scale_first * branch

    weight_hidden = (
        dense_full[:, : parts * shard]
        .reshape(count, parts, shard, width)
        .transpose(0, 2, 1, 3)
        .reshape(width, ff)
    )
    weight_project = dense_full[:, parts * shard :].reshape(ff, width)
    normed_two, second_norm_back = jax.vjp(layer_norm, middle, gain_second, bias_second)
    normed_two_low = normed_two.astype(bf16)
    hidden = product(normed_two_low, weight_hidden) + bias_hidden
    active, gelu_back = jax.vjp(gelu_exact, hidden)
    active_low = active.astype(bf16)
    dense_out = product(active_low, weight_project) + bias_project
    layer_output = (middle + scale_second * dense_out).astype(bf16)
    upstream = cotangent.astype(f32)
    dense_scale_grad = jnp.sum(upstream * dense_out, axis=0)
    grad_dense = (upstream * scale_second).astype(bf16)
    project_weight_grad = inner_rows(active_low, grad_dense).astype(bf16)
    project_bias_grad = column_sums(grad_dense)
    grad_hidden = gelu_back(against(grad_dense, weight_project))[0].astype(bf16)
    hidden_weight_grad = inner_rows(normed_two_low, grad_hidden).astype(bf16)
    hidden_bias_grad = column_sums(grad_hidden)
    grad_middle_norm, second_gain_grad, second_bias_grad = second_norm_back(against(grad_hidden, weight_hidden))
    grad_middle = upstream + grad_middle_norm
    attention_scale_grad = jnp.sum(grad_middle * branch, axis=0)
    grad_branch = (grad_middle * scale_first).astype(bf16)
    output_weight_grad = inner_rows(attended_low, grad_branch).astype(bf16)
    output_bias_grad = column_sums(grad_branch)
    grad_attended = against(grad_branch, weight_output).astype(bf16)

    bits = list(range(depth - 1, -1, -1))
    project_rows = project_weight_grad.shape[0] // count
    cut = 3 * width // 4
    part_a = bit_view(project_weight_grad[:, :cut], count, project_rows)
    part_b = bit_view(hidden_weight_grad[:, :3 * width], count, shard)
    rest = project_weight_grad[:, cut:].reshape(count, parts, shard, width - cut)
    part_c = jnp.concatenate(
        [rest[:, j] for j in range(parts)]
        + [
            hidden_weight_grad[:, 3 * width :].reshape(count, shard, -1),
            output_weight_grad.reshape(count, shard, width),
        ],
        axis=2,
    )
    part_c = part_c.reshape((2,) * depth + part_c.shape[1:])

    def order_of(turn, low):
        chips = list(range(1, depth))
        axes, last = chips[:3], chips[3:]
        return low + axes[turn:] + axes[:turn] + last

    sum_a = scatter_sum(part_a, bits, order_of(0, [0]))
    sum_b = scatter_sum(part_b, bits, order_of(1, [0]))
    sum_c = scatter_sum(part_c, bits, order_of(2, [0]))

    grad_half = jnp.where(core == 0, grad_attended[:, :half], grad_attended[:, half:])
    grad_other = swap(jnp.where(core == 0, grad_attended[:, half:], grad_attended[:, :half]), 0)
    grad_pair = jnp.where(
        core == 0, jnp.concatenate([grad_half, grad_other]), jnp.concatenate([grad_other, grad_half])
    )
    delta = jnp.sum((grad_pair.astype(f32) * attended_f).reshape(2 * rows, 2 * pairs, HEAD_DIM), axis=2)
    stats = jnp.concatenate([lse.reshape(2 * rows, 2 * pairs, HEAD_DIM)[:, :, 0].T, delta.T])
    top = lax.reduce_precision(stats, 8, 7)
    mid = lax.reduce_precision(stats - top, 8, 7)
    pieces = jnp.concatenate([top, mid, stats - top - mid]).astype(bf16)
    stat_count = pieces.shape[0]
    packed = [jnp.concatenate([grad_pair[c * rows : (c + 1) * rows], pieces[:, c * rows : (c + 1) * rows]]) for c in range(2)]
    both = jnp.concatenate(packed)
    from_below = shifted(both, 2)
    from_above = shifted(both, -2)
    far_below = shifted(packed[1], 4)
    far_above = shifted(packed[0], -4)
    unit = rows + stat_count
    arrived = [far_below, from_below[:unit], from_below[unit:], packed[0], packed[1], from_above[:unit], from_above[unit:], far_above]
    grad_window = jnp.concatenate([b[:rows] for b in arrived])
    stat_window = jnp.concatenate([b[rows:] for b in arrived], axis=1).astype(f32)
    stat_window = stat_window.reshape(3, 2, pairs, 2, window)
    stat_window = (stat_window[0] + stat_window[1] + stat_window[2]).transpose(1, 0, 2, 3).reshape(pairs, 4, window)
    delta_wide = jnp.repeat(delta, HEAD_DIM, axis=1)
    (grad_queries,) = attention_call(
        partial(query_kernel, first),
        grid,
        [q_own, k_all, v_all, label_rows, label_all, row_block, row_block, row_block],
        [row_block],
        [jax.ShapeDtypeStruct((2 * rows, half), bf16)],
        [pltpu.VMEM((2, BLK, PAIR), f32)],
        3 * share,
    )(lo, hi, projected, projected, projected, query_label[:, None], key_label[None], grad_pair, lse, delta_wide)
    stat_spec = pl.BlockSpec((1, 4, window), lambda h, b, lo, hi: (h, 0, 0))
    do_all = pl.BlockSpec((window, PAIR), lambda h, b, lo, hi: (0, h))
    grad_keys, grad_values = attention_call(
        partial(key_kernel, first),
        grid,
        [q_all, k_own, v_own, label_all, label_rows, do_all, stat_spec],
        [row_block, row_block],
        [jax.ShapeDtypeStruct((2 * rows, half), bf16)] * 2,
        [pltpu.VMEM((2, BLK, PAIR), f32)] * 2,
        4 * share,
    )(lo, hi, projected, projected, projected, query_label[None], key_label[:, None], grad_window, stat_window)

    normed_pair = normed_window[first_row:last_row]
    chip_bits = bits[:-1]
    sums = [
        scatter_sum(inner_rows(normed_pair, g).astype(bf16).reshape((2,) * (depth - 1) + (2 * shard, half)), chip_bits, order_of(turn, []))
        for turn, g in enumerate((grad_queries, grad_keys, grad_values))
    ]
    chip_rows = jnp.concatenate(sums, axis=1)
    kept = lax.dynamic_slice_in_dim(chip_rows, core * shard, shard, 0)
    other = swap(lax.dynamic_slice_in_dim(chip_rows, (1 - core) * shard, shard, 0), 0)
    query_out, key_out, value_out = [
        columns_of(core, kept[:, i * half : (i + 1) * half], other[:, i * half : (i + 1) * half]).astype(f32)
        for i in range(3)
    ]

    grad_all = jnp.concatenate([grad_queries, grad_keys, grad_values], axis=1)
    grad_normed_pair = against(grad_all, weight_qkv)
    grad_normed = lax.dynamic_slice_in_dim(grad_normed_pair, core * rows, rows, 0) + swap(
        lax.dynamic_slice_in_dim(grad_normed_pair, (1 - core) * rows, rows, 0), 0
    )
    _, first_norm_back = jax.vjp(layer_norm, inputs, gain_first, bias_first)
    grad_input_norm, first_gain_grad, first_bias_grad = first_norm_back(grad_normed)
    input_gradient = grad_middle + grad_input_norm

    def placed_half(values):
        spread = jnp.zeros((width,), f32)
        return lax.dynamic_update_slice_in_dim(spread, values, core * half, 0)

    grads = [
        first_gain_grad,
        first_bias_grad,
        placed_half(column_sums(grad_queries)),
        placed_half(column_sums(grad_values)),
        output_bias_grad,
        attention_scale_grad,
        second_gain_grad,
        second_bias_grad,
        project_bias_grad,
        dense_scale_grad,
        hidden_bias_grad,
    ]
    vector_rows = jnp.concatenate([g.reshape(count, -1) for g in grads], axis=1)
    vector_rows = jnp.pad(vector_rows, ((0, 0), (0, -vector_rows.shape[1] % 128)))
    vector_sum = scatter_sum(vector_rows.reshape((2,) * depth + (1, -1)), bits, bits, f32)[0]
    out = [vector_sum[i * shard : (i + 1) * shard] for i in range(10)]
    hidden_bias_out = vector_sum[10 * shard : (10 + parts) * shard]
    c_rows = sum_c.astype(f32)
    rest_width = width - cut
    project_out = jnp.concatenate(
        [sum_a.astype(f32), jnp.concatenate([c_rows[:, j * rest_width : (j + 1) * rest_width] for j in range(parts)])], axis=1
    )
    hidden_out = jnp.concatenate([sum_b.astype(f32), c_rows[:, width : 2 * width]], axis=1)
    output_out = c_rows[:, 2 * width :]
    return (
        layer_output,
        input_gradient,
        out[0],
        out[1],
        query_out,
        out[2],
        key_out,
        value_out,
        out[3],
        output_out,
        out[4],
        out[5],
        out[6],
        out[7],
        hidden_out,
        hidden_bias_out,
        project_out,
        out[8],
        out[9],
    )


def solution(mesh):
    placed = (
        P("dev", None),
        P("dev", None),
        P("dev"),
        P("dev"),
        P("dev"),
        P("dev"),
        P("dev", None),
        P("dev"),
        P("dev", None),
        P("dev", None),
        P("dev"),
        P("dev", None),
        P("dev"),
        P("dev"),
        P("dev"),
        P("dev"),
        P("dev", None),
        P("dev"),
        P("dev", None),
        P("dev"),
        P("dev"),
    )
    return jax.shard_map(
        on_device,
        mesh=mesh,
        in_specs=placed,
        out_specs=(
            P("dev", None),
            P("dev", None),
            P("dev"),
            P("dev"),
            P("dev", None),
            P("dev"),
            P("dev", None),
            P("dev", None),
            P("dev"),
            P("dev", None),
            P("dev"),
            P("dev"),
            P("dev"),
            P("dev"),
            P("dev", None),
            P("dev"),
            P("dev", None),
            P("dev"),
            P("dev"),
        ),
        check_vma=False,
    )
```

```python
from functools import partial
import jax
import jax.numpy as jnp
from jax import lax
from jax.experimental import pallas as pl
from jax.experimental.pallas import tpu as pltpu
from jax.sharding import PartitionSpec as P

HEAD_DIM = 64
PAIR = 2 * HEAD_DIM
IMG = 1370
BLK = 256
STEP = 512
norm_eps = 1e-06
bf16 = jnp.bfloat16
f32 = jnp.float32
NEG = -1e30


def layer_norm(row_values, gain_row, bias_row):
    center = row_values - jnp.mean(row_values, axis=-1, keepdims=True)
    spread = jnp.mean(center * center, axis=-1, keepdims=True)
    return center * lax.rsqrt(spread + norm_eps) * gain_row + bias_row


def product(a, b):
    return jnp.dot(a, b, preferred_element_type=f32)


def inner_rows(a, b):
    return lax.dot_general(a, b, (((0,), (0,)), ((), ())), preferred_element_type=f32)


def against(a, b):
    return lax.dot_general(a, b, (((1,), (1,)), ((), ())), preferred_element_type=f32)


def column_sums(rows):
    return jnp.sum(rows.astype(f32), axis=0)


def head_lanes(h):
    lane = lax.broadcasted_iota(jnp.int32, (1, PAIR), 1)
    return (lane >= h * HEAD_DIM) & (lane < (h + 1) * HEAD_DIM)


def own_head(block, h):
    return jnp.where(head_lanes(h), block, jnp.zeros_like(block))


def steps_of(lo, hi, block, window):
    per = STEP // BLK
    steps = (hi[block] - lo[block] + per - 1) // per
    return jnp.minimum(lo[block], window // BLK - per * steps), steps


def apart_of():
    shape = (BLK, STEP)
    return lax.broadcasted_iota(jnp.int32, shape, 1) - lax.broadcasted_iota(jnp.int32, shape, 0)


def step_rows(start, step):
    block = start + step * (STEP // BLK)
    return block, pl.ds(pl.multiple_of(block * BLK, BLK), STEP)


def folded(combine, block):
    parts = [block[:, i : i + 128] for i in range(0, block.shape[1], 128)]
    while len(parts) > 1:
        parts = [combine(parts[i], parts[i + 1]) for i in range(0, len(parts), 2)]
    return parts[0]


def attend_kernel(first, lo, hi, q_ref, k_ref, v_ref, ql_ref, kl_ref, o_ref, lse_ref, s_ref, m_ref, l_ref, a_ref):
    block = pl.program_id(1)
    start, steps = steps_of(lo, hi, block, k_ref.shape[0])
    apart = apart_of()
    ql = ql_ref[...]
    heads = [own_head(q_ref[...], h) for h in range(2)]
    m_ref[...] = jnp.full(m_ref.shape, NEG, f32)
    l_ref[...] = jnp.zeros(l_ref.shape, f32)
    a_ref[...] = jnp.zeros(a_ref.shape, f32)

    def scores(step, _):
        kb, rows = step_rows(start, step)
        k = k_ref[rows, :]
        seen = (ql == kl_ref[:, rows]) | (apart == (first + block - kb) * BLK)
        for h in range(2):
            s = jnp.where(seen, against(heads[h], k), NEG)
            s_ref[h, step] = s
            m_ref[h] = jnp.maximum(m_ref[h], folded(jnp.maximum, s))
        return 0

    lax.fori_loop(0, steps, scores, 0)
    peaks = [jnp.max(m_ref[h], axis=1, keepdims=True) for h in range(2)]

    def values(step, _):
        _, rows = step_rows(start, step)
        v = v_ref[rows, :]
        for h in range(2):
            p = jnp.exp(s_ref[h, step] - peaks[h])
            l_ref[h] = l_ref[h] + folded(jnp.add, p)
            a_ref[h] = a_ref[h] + product(p.astype(bf16), v)
        return 0

    lax.fori_loop(0, steps, values, 0)
    totals = [jnp.sum(l_ref[h], axis=1, keepdims=True) for h in range(2)]
    first_head = head_lanes(0)
    o_ref[...] = jnp.where(first_head, a_ref[0] / totals[0], a_ref[1] / totals[1])
    lse_ref[...] = jnp.where(first_head, peaks[0] + jnp.log(totals[0]), peaks[1] + jnp.log(totals[1]))


def query_kernel(first, lo, hi, q_ref, k_ref, v_ref, ql_ref, kl_ref, do_ref, lse_ref, dl_ref, dq_ref, a_ref):
    block = pl.program_id(1)
    start, steps = steps_of(lo, hi, block, k_ref.shape[0])
    apart = apart_of()
    ql = ql_ref[...]
    q = [own_head(q_ref[...], h) for h in range(2)]
    do = [own_head(do_ref[...], h) for h in range(2)]
    lse = [lse_ref[:, h * HEAD_DIM : h * HEAD_DIM + 1] for h in range(2)]
    delta = [dl_ref[:, h * HEAD_DIM : h * HEAD_DIM + 1] for h in range(2)]
    a_ref[...] = jnp.zeros(a_ref.shape, f32)

    def take(step, _):
        kb, rows = step_rows(start, step)
        k = k_ref[rows, :]
        v = v_ref[rows, :]
        seen = (ql == kl_ref[:, rows]) | (apart == (first + block - kb) * BLK)
        for h in range(2):
            p = jnp.exp(jnp.where(seen, against(q[h], k), NEG) - lse[h])
            ds = (p * (against(do[h], v) - delta[h])).astype(bf16)
            a_ref[h] = a_ref[h] + product(ds, k)
        return 0

    lax.fori_loop(0, steps, take, 0)
    dq_ref[...] = (jnp.where(head_lanes(0), a_ref[0], a_ref[1]) * (HEAD_DIM**-0.5)).astype(bf16)


def key_kernel(first, lo, hi, q_ref, k_ref, v_ref, ql_ref, kl_ref, do_ref, st_ref, dk_ref, dv_ref, a_ref, b_ref):
    block = pl.program_id(1)
    start, steps = steps_of(lo, hi, block, q_ref.shape[0])
    apart = apart_of()
    kl = kl_ref[...]
    k = [own_head(k_ref[...], h) for h in range(2)]
    v = [own_head(v_ref[...], h) for h in range(2)]
    a_ref[...] = jnp.zeros(a_ref.shape, f32)
    b_ref[...] = jnp.zeros(b_ref.shape, f32)

    def take(step, _):
        qb, rows = step_rows(start, step)
        q = q_ref[rows, :]
        do = do_ref[rows, :]
        seen = (kl == ql_ref[:, rows]) | (apart == (first + block - qb) * BLK)
        for h in range(2):
            lse = st_ref[0, h : h + 1, rows]
            delta = st_ref[0, 2 + h : 3 + h, rows]
            p = jnp.exp(jnp.where(seen, against(k[h], q), NEG) - lse)
            ds = (p * (against(v[h], do) - delta)).astype(bf16)
            a_ref[h] = a_ref[h] + product(ds, q)
            b_ref[h] = b_ref[h] + product(p.astype(bf16), do)
        return 0

    lax.fori_loop(0, steps, take, 0)
    dk_ref[...] = jnp.where(head_lanes(0), a_ref[0], a_ref[1]).astype(bf16)
    dv_ref[...] = jnp.where(head_lanes(0), b_ref[0], b_ref[1]).astype(bf16)


def dense_kernel(
    n_ref, gd_ref, wh_ref, wp_ref, bh_ref, out_ref, gn_ref, dw_ref, dbh_ref, act_ref, gh_ref
):
    @pl.when(pl.program_id(0) == 0)
    def _():
        out_ref[...] = jnp.zeros(out_ref.shape, f32)
        gn_ref[...] = jnp.zeros(gn_ref.shape, f32)

    n = n_ref[...]
    gd = gd_ref[...]
    for u in range(0, wh_ref.shape[2], BLK):
        units = slice(u, u + BLK)
        hidden = product(n, wh_ref[0, :, units]) + bh_ref[0, :, units]
        grad = against(gd, wp_ref[0, units, :])
        below = 0.5 + 0.5 * lax.erf(hidden * 0.7071067811865476)
        act_ref[:, units] = (hidden * below).astype(bf16)
        gh = grad * (below + hidden * (jnp.exp(-0.5 * hidden * hidden) * 0.3989422804014327))
        gh_low = gh.astype(bf16)
        gh_ref[:, units] = gh_low
        dbh_ref[0, :, units] = jnp.sum(gh_low.astype(f32), axis=0, keepdims=True)
        dw_ref[1, 0, units, :] = inner_rows(act_ref[:, units], gd).astype(bf16)
        dw_ref[0, 0, :, units] = inner_rows(n, gh_low).astype(bf16)
    out_ref[...] += product(act_ref[...], wp_ref[0])
    gn_ref[...] += against(gh_ref[...], wh_ref[0])


def dense_call(n, gd, weights, bias):
    rows, width = n.shape
    parts = weights.shape[0] // 2
    whole = pl.BlockSpec((rows, width), lambda j: (0, 0))
    chunk = pl.BlockSpec((1, width, width), lambda j: (j, 0, 0))
    second = pl.BlockSpec((1, width, width), lambda j: (parts + j, 0, 0))
    row = pl.BlockSpec((1, 1, width), lambda j: (j, 0, 0))
    return pl.pallas_call(
        dense_kernel,
        grid=(parts,),
        in_specs=[whole, whole, chunk, second, row],
        out_specs=[whole, whole, pl.BlockSpec((2, 1, width, width), lambda j: (0, j, 0, 0)), row],
        out_shape=[
            jax.ShapeDtypeStruct((rows, width), f32),
            jax.ShapeDtypeStruct((rows, width), f32),
            jax.ShapeDtypeStruct((2, parts, width, width), bf16),
            jax.ShapeDtypeStruct((parts, 1, width), f32),
        ],
        scratch_shapes=[pltpu.VMEM((rows, width), bf16)] * 2,
        compiler_params=pltpu.CompilerParams(vmem_limit_bytes=56 * 1024 * 1024),
        cost_estimate=pl.CostEstimate(flops=50_000_000_000, bytes_accessed=40_000_000, transcendentals=4_000_000),
    )(n, gd, weights, weights, bias)


def attention_call(kernel, grid, in_specs, out_specs, out_shape, scratch, flops):
    return pl.pallas_call(
        kernel,
        grid_spec=pltpu.PrefetchScalarGridSpec(
            num_scalar_prefetch=2,
            grid=grid,
            in_specs=in_specs,
            out_specs=out_specs,
            scratch_shapes=scratch,
        ),
        out_shape=out_shape,
        compiler_params=pltpu.CompilerParams(vmem_limit_bytes=48 * 1024 * 1024),
        cost_estimate=pl.CostEstimate(flops=flops, bytes_accessed=8_000_000, transcendentals=0),
    )


def own_bit(bit):
    return (lax.axis_index("dev") >> bit) & 1


def swap(block, bit):
    count = lax.axis_size("dev")
    return lax.ppermute(block, "dev", [(i, i ^ (1 << bit)) for i in range(count)])


def shifted(block, distance):
    count = lax.axis_size("dev")
    return lax.ppermute(block, "dev", [(i, i + distance) for i in range(count) if 0 <= i + distance < count])


def pick(block, axis, index):
    return lax.dynamic_index_in_dim(block, index, axis, keepdims=False)


def scatter_sum(blocks, bits, order, kind=bf16):
    bits = list(bits)
    for bit in order:
        axis = bits.index(bit)
        mine = own_bit(bit)
        sent = jnp.concatenate([pick(b, axis, 1 - mine) for b in blocks], axis=-2).astype(kind)
        kept = jnp.concatenate([pick(b, axis, mine) for b in blocks], axis=-2)
        block = kept.astype(f32) + swap(sent, bit).astype(f32)
        blocks = [block.astype(kind)]
        bits.remove(bit)
    return blocks[0]


def on_device(
    tokens,
    cotangent,
    segment_ids,
    validity,
    first_gain,
    first_bias,
    query_weight,
    query_bias,
    key_weight,
    value_weight,
    value_bias,
    output_weight,
    output_bias,
    attention_scale,
    second_gain,
    second_bias,
    hidden_weight,
    hidden_bias,
    project_weight,
    project_bias,
    dense_scale,
):
    count = lax.axis_size("dev")
    depth = count.bit_length() - 1
    rows, width = tokens.shape
    half = width // 2
    window = 8 * rows
    assert 1 << depth == count and 2 * rows + rows >= IMG - 1 and rows % BLK == 0
    core = own_bit(0)
    shard = query_weight.shape[0]
    ff = hidden_weight.shape[1]
    parts = ff // width

    vectors = jnp.concatenate(
        [
            v.reshape(-1, shard).T
            for v in (
                first_gain,
                first_bias,
                query_bias,
                value_bias,
                output_bias,
                attention_scale,
                second_gain,
                second_bias,
                project_bias,
                dense_scale,
                hidden_bias,
            )
        ],
        axis=1,
    )
    vectors = jnp.pad(vectors, ((0, 0), (0, 128 - vectors.shape[1])))
    attention_pack = jnp.concatenate(
        [w[:, c * half : (c + 1) * half] for c in range(2) for w in (query_weight, key_weight, value_weight)]
        + [output_weight, vectors],
        axis=1,
    )
    hidden_local = hidden_weight.reshape(shard, count, parts, shard).transpose(2, 0, 1, 3).reshape(parts, shard, width)
    dense_pack = jnp.concatenate([hidden_local, project_weight.reshape(parts, shard, width)])
    attention_full = lax.all_gather(attention_pack, "dev", axis=0, tiled=True)
    dense_full = lax.all_gather(dense_pack, "dev", axis=1, tiled=True)

    labels = segment_ids + 1
    tag_rows = jnp.stack(
        [jnp.concatenate([labels % 256, labels // 256]), jnp.concatenate([validity, jnp.zeros_like(validity)])]
    ).astype(bf16)
    tag_rows = jnp.pad(tag_rows, ((0, 14), (0, 0)))
    own = jnp.concatenate([tokens, tag_rows])
    below = shifted(own, 2)
    above = shifted(own, -2)
    far = lax.ppermute(
        own,
        "dev",
        [(i, i - 4) for i in range(4, count, 2)] + [(i, i + 4) for i in range(1, count - 4, 2)],
    )
    mine = jnp.stack([below, own, above, far])
    theirs = swap(mine, 0)
    zero, one = jnp.where(core == 0, mine, theirs), jnp.where(core == 0, theirs, mine)
    blocks = [one[3], zero[0], one[0], zero[1], one[1], zero[2], one[2], zero[3]]
    window_tokens = jnp.concatenate([b[:rows] for b in blocks])
    tags = jnp.stack([b[rows : rows + 2] for b in blocks]).astype(jnp.int32)
    window_labels = (tags[:, 0, :rows] + 256 * tags[:, 0, rows:]).reshape(window)
    window_valid = tags[:, 1, :rows].reshape(window)
    key_label = jnp.where(window_valid == 1, window_labels, 0)
    query_label = jnp.where(window_labels == 0, -1, window_labels)
    first_row, last_row = 3 * rows, 5 * rows
    own_blocks = 2 * rows // BLK
    index = lax.broadcasted_iota(jnp.int32, (own_blocks, window), 1)
    block_labels = window_labels[first_row:last_row].reshape(own_blocks, BLK)
    lo = jnp.min(jnp.where(window_labels[None] == block_labels[:, :1], index, window), axis=1) // BLK
    hi = jnp.max(jnp.where(window_labels[None] == block_labels[:, -1:], index, -1), axis=1) // BLK + 1

    columns = attention_full[:, 4 * width :].T.astype(f32)
    (
        gain_first,
        bias_first,
        bias_query,
        bias_value,
        bias_output,
        scale_first,
        gain_second,
        bias_second,
        bias_project,
        scale_second,
    ) = [columns[i] for i in range(10)]
    bias_hidden = columns[10 : 10 + parts].reshape(parts, 1, width)
    weight_qkv = lax.dynamic_slice_in_dim(attention_full, core * 3 * half, 3 * half, 1)
    weight_output = attention_full[:, 3 * width : 4 * width]

    normed_window = layer_norm(window_tokens.astype(f32), gain_first, bias_first).astype(bf16)
    start = core * half
    bias_qkv = jnp.concatenate(
        [
            lax.dynamic_slice_in_dim(bias_query, start, half),
            jnp.zeros((half,), f32),
            lax.dynamic_slice_in_dim(bias_value, start, half),
        ]
    )
    scale_qkv = jnp.concatenate([jnp.full((half,), HEAD_DIM**-0.5, f32), jnp.ones((2 * half,), f32)])
    projected = ((product(normed_window, weight_qkv) + bias_qkv) * scale_qkv).astype(bf16)

    pairs = half // PAIR
    first = first_row // BLK

    def own_rows(group):
        return pl.BlockSpec((BLK, PAIR), lambda h, b, lo, hi: (first + b, group * pairs + h))

    def all_rows(group):
        return pl.BlockSpec((window, PAIR), lambda h, b, lo, hi: (0, group * pairs + h))

    row_block = pl.BlockSpec((BLK, PAIR), lambda h, b, lo, hi: (b, h))
    label_rows = pl.BlockSpec((BLK, 1), lambda h, b, lo, hi: (first + b, 0))
    label_all = pl.BlockSpec((1, window), lambda h, b, lo, hi: (0, 0))
    attended_f, lse = attention_call(
        partial(attend_kernel, first),
        (pairs, own_blocks),
        [own_rows(0), all_rows(1), all_rows(2), label_rows, label_all],
        [row_block, row_block],
        [jax.ShapeDtypeStruct((2 * rows, half), f32)] * 2,
        [
            pltpu.VMEM((2, window // STEP, BLK, STEP), f32),
            pltpu.VMEM((2, BLK, 128), f32),
            pltpu.VMEM((2, BLK, 128), f32),
            pltpu.VMEM((2, BLK, PAIR), f32),
        ],
        60_000_000_000,
    )(lo, hi, projected, projected, projected, query_label[:, None], key_label[None])

    def columns_of(c, mine, theirs):
        return jnp.where(c == 0, jnp.concatenate([mine, theirs], 1), jnp.concatenate([theirs, mine], 1))

    attended_half = attended_f.astype(bf16)
    attended_low = columns_of(
        core,
        lax.dynamic_slice_in_dim(attended_half, core * rows, rows, 0),
        swap(lax.dynamic_slice_in_dim(attended_half, (1 - core) * rows, rows, 0), 0),
    )
    inputs = tokens.astype(f32)
    branch = product(attended_low, weight_output) + bias_output
    middle = inputs + scale_first * branch

    normed_two, second_norm_back = jax.vjp(layer_norm, middle, gain_second, bias_second)
    upstream = cotangent.astype(f32)
    grad_dense = (upstream * scale_second).astype(bf16)
    dense_sum, grad_normed_two, dense_weight_grads, hidden_bias_grad = dense_call(
        normed_two.astype(bf16), grad_dense, dense_full, bias_hidden
    )
    dense_out = dense_sum + bias_project
    layer_output = (middle + scale_second * dense_out).astype(bf16)
    dense_scale_grad = jnp.sum(upstream * dense_out, axis=0)
    project_bias_grad = column_sums(grad_dense)
    grad_middle_norm, second_gain_grad, second_bias_grad = second_norm_back(grad_normed_two)
    grad_middle = upstream + grad_middle_norm
    attention_scale_grad = jnp.sum(grad_middle * branch, axis=0)
    grad_branch = (grad_middle * scale_first).astype(bf16)
    output_weight_grad = inner_rows(attended_low, grad_branch).astype(bf16)
    output_bias_grad = column_sums(grad_branch)
    grad_attended = against(grad_branch, weight_output).astype(bf16)

    dense_sums = lax.psum_scatter(
        dense_weight_grads.reshape(2 * parts, width, width), "dev", scatter_dimension=1, tiled=True
    )
    bits = list(range(depth - 1, -1, -1))

    def order_of(turn, low):
        chips = list(range(1, depth))
        axes, last = chips[:3], chips[3:]
        return low + axes[turn:] + axes[:turn] + last

    output_sum = scatter_sum([output_weight_grad.reshape((2,) * depth + (shard, width))], bits, order_of(2, [0]))

    grad_half = jnp.where(core == 0, grad_attended[:, :half], grad_attended[:, half:])
    grad_other = swap(jnp.where(core == 0, grad_attended[:, half:], grad_attended[:, :half]), 0)
    grad_pair = jnp.where(
        core == 0, jnp.concatenate([grad_half, grad_other]), jnp.concatenate([grad_other, grad_half])
    )
    delta = jnp.sum((grad_pair.astype(f32) * attended_f).reshape(2 * rows, 2 * pairs, HEAD_DIM), axis=2)
    stats = jnp.concatenate([lse.reshape(2 * rows, 2 * pairs, HEAD_DIM)[:, :, 0].T, delta.T])
    top = lax.reduce_precision(stats, 8, 7)
    mid = lax.reduce_precision(stats - top, 8, 7)
    pieces = jnp.concatenate([top, mid, stats - top - mid]).astype(bf16)
    stat_count = pieces.shape[0]
    packed = [jnp.concatenate([grad_pair[c * rows : (c + 1) * rows], pieces[:, c * rows : (c + 1) * rows]]) for c in range(2)]
    both = jnp.concatenate(packed)
    from_below = shifted(both, 2)
    from_above = shifted(both, -2)
    far_below = shifted(packed[1], 4)
    far_above = shifted(packed[0], -4)
    delta_wide = jnp.repeat(delta, HEAD_DIM, axis=1)
    (grad_queries,) = attention_call(
        partial(query_kernel, first),
        (pairs, own_blocks),
        [own_rows(0), all_rows(1), all_rows(2), label_rows, label_all, row_block, row_block, row_block],
        [row_block],
        [jax.ShapeDtypeStruct((2 * rows, half), bf16)],
        [pltpu.VMEM((2, BLK, PAIR), f32)],
        60_000_000_000,
    )(lo, hi, projected, projected, projected, query_label[:, None], key_label[None], grad_pair, lse, delta_wide)
    from_below, from_above, far_below, far_above, grad_queries = lax.optimization_barrier(
        (from_below, from_above, far_below, far_above, grad_queries)
    )
    unit = rows + stat_count
    arrived = [far_below, from_below[:unit], from_below[unit:], packed[0], packed[1], from_above[:unit], from_above[unit:], far_above]
    grad_window = jnp.concatenate([b[:rows] for b in arrived])
    stat_window = jnp.concatenate([b[rows:] for b in arrived], axis=1).astype(f32)
    stat_window = stat_window.reshape(3, 2, pairs, 2, window)
    stat_window = (stat_window[0] + stat_window[1] + stat_window[2]).transpose(1, 0, 2, 3).reshape(pairs, 4, window)
    grad_keys, grad_values = attention_call(
        partial(key_kernel, first),
        (pairs, own_blocks),
        [
            all_rows(0),
            own_rows(1),
            own_rows(2),
            label_all,
            label_rows,
            pl.BlockSpec((window, PAIR), lambda h, b, lo, hi: (0, h)),
            pl.BlockSpec((1, 4, window), lambda h, b, lo, hi: (h, 0, 0)),
        ],
        [row_block, row_block],
        [jax.ShapeDtypeStruct((2 * rows, half), bf16)] * 2,
        [pltpu.VMEM((2, BLK, PAIR), f32)] * 2,
        70_000_000_000,
    )(lo, hi, projected, projected, projected, query_label[None], key_label[:, None], grad_window, stat_window)

    normed_pair = normed_window[first_row:last_row]
    chip_bits = bits[:-1]
    sums = [
        scatter_sum([inner_rows(normed_pair, g).astype(bf16).reshape((2,) * (depth - 1) + (2 * shard, half))], chip_bits, order_of(turn, []))
        for turn, g in enumerate((grad_queries, grad_keys, grad_values))
    ]
    chip_rows = jnp.concatenate(sums, axis=1)
    kept = lax.dynamic_slice_in_dim(chip_rows, core * shard, shard, 0)
    other = swap(lax.dynamic_slice_in_dim(chip_rows, (1 - core) * shard, shard, 0), 0)
    query_out, key_out, value_out = [
        columns_of(core, kept[:, i * half : (i + 1) * half], other[:, i * half : (i + 1) * half]).astype(f32)
        for i in range(3)
    ]

    grad_all = jnp.concatenate([grad_queries, grad_keys, grad_values], axis=1)
    grad_normed_pair = against(grad_all, weight_qkv)
    grad_normed = lax.dynamic_slice_in_dim(grad_normed_pair, core * rows, rows, 0) + swap(
        lax.dynamic_slice_in_dim(grad_normed_pair, (1 - core) * rows, rows, 0), 0
    )
    _, first_norm_back = jax.vjp(layer_norm, inputs, gain_first, bias_first)
    grad_input_norm, first_gain_grad, first_bias_grad = first_norm_back(grad_normed)
    input_gradient = grad_middle + grad_input_norm

    def placed_half(values):
        spread = jnp.zeros((width,), f32)
        return lax.dynamic_update_slice_in_dim(spread, values, core * half, 0)

    grads = [
        first_gain_grad,
        first_bias_grad,
        placed_half(column_sums(grad_queries)),
        placed_half(column_sums(grad_values)),
        output_bias_grad,
        attention_scale_grad,
        second_gain_grad,
        second_bias_grad,
        project_bias_grad,
        dense_scale_grad,
        hidden_bias_grad.reshape(parts, count, shard).transpose(1, 0, 2),
    ]
    vector_rows = jnp.concatenate([g.reshape(count, -1) for g in grads], axis=1)
    vector_rows = jnp.pad(vector_rows, ((0, 0), (0, -vector_rows.shape[1] % 128)))
    vector_sum = scatter_sum([vector_rows.reshape((2,) * depth + (1, -1))], bits, bits, f32)[0]
    out = [vector_sum[i * shard : (i + 1) * shard] for i in range(10)]
    hidden_bias_out = vector_sum[10 * shard : (10 + parts) * shard]
    dense_sums = dense_sums.astype(f32)
    project_out = dense_sums[parts:].reshape(parts * shard, width)
    hidden_out = dense_sums[:parts].reshape(parts, shard, count, shard).transpose(1, 2, 0, 3).reshape(shard, ff)
    output_out = output_sum.astype(f32)
    return (
        layer_output,
        input_gradient,
        out[0],
        out[1],
        query_out,
        out[2],
        key_out,
        value_out,
        out[3],
        output_out,
        out[4],
        out[5],
        out[6],
        out[7],
        hidden_out,
        hidden_bias_out,
        project_out,
        out[8],
        out[9],
    )


def solution(mesh):
    placed = (
        P("dev", None),
        P("dev", None),
        P("dev"),
        P("dev"),
        P("dev"),
        P("dev"),
        P("dev", None),
        P("dev"),
        P("dev", None),
        P("dev", None),
        P("dev"),
        P("dev", None),
        P("dev"),
        P("dev"),
        P("dev"),
        P("dev"),
        P("dev", None),
        P("dev"),
        P("dev", None),
        P("dev"),
        P("dev"),
    )
    return jax.shard_map(
        on_device,
        mesh=mesh,
        in_specs=placed,
        out_specs=(
            P("dev", None),
            P("dev", None),
            P("dev"),
            P("dev"),
            P("dev", None),
            P("dev"),
            P("dev", None),
            P("dev", None),
            P("dev"),
            P("dev", None),
            P("dev"),
            P("dev"),
            P("dev"),
            P("dev"),
            P("dev", None),
            P("dev"),
            P("dev", None),
            P("dev"),
            P("dev"),
        ),
        check_vma=False,
    )
```

```python
from functools import partial
import jax
import jax.numpy as jnp
from jax import lax
from jax.experimental import pallas as pl
from jax.experimental.pallas import tpu as pltpu
from jax.sharding import PartitionSpec as P

HEAD_DIM = 64
PAIR = 2 * HEAD_DIM
IMG = 1370
BLK = 256
STEP = 512
norm_eps = 1e-06
bf16 = jnp.bfloat16
f32 = jnp.float32
NEG = -1e30


def layer_norm(row_values, gain_row, bias_row):
    center = row_values - jnp.mean(row_values, axis=-1, keepdims=True)
    spread = jnp.mean(center * center, axis=-1, keepdims=True)
    return center * lax.rsqrt(spread + norm_eps) * gain_row + bias_row


def product(a, b):
    return jnp.dot(a, b, preferred_element_type=f32)


def inner_rows(a, b):
    return lax.dot_general(a, b, (((0,), (0,)), ((), ())), preferred_element_type=f32)


def against(a, b):
    return lax.dot_general(a, b, (((1,), (1,)), ((), ())), preferred_element_type=f32)


def column_sums(rows):
    return jnp.sum(rows.astype(f32), axis=0)


def head_lanes(h):
    lane = lax.broadcasted_iota(jnp.int32, (1, PAIR), 1)
    return (lane >= h * HEAD_DIM) & (lane < (h + 1) * HEAD_DIM)


def own_head(block, h):
    return jnp.where(head_lanes(h), block, jnp.zeros_like(block))


def over_range(body, lo, hi, block):
    per = STEP // BLK
    start, count = lo[block], hi[block] - lo[block]
    steps = count // per

    def take(step, carried):
        body(start + per * step, step, STEP)
        return carried

    lax.fori_loop(0, steps, take, 0)

    @pl.when(count % per > 0)
    def _():
        body(start + per * steps, steps, BLK)


def apart_of():
    shape = (BLK, STEP)
    return lax.broadcasted_iota(jnp.int32, shape, 1) - lax.broadcasted_iota(jnp.int32, shape, 0)


def block_rows(block, size):
    return pl.ds(pl.multiple_of(block * BLK, BLK), size)


def heads_of(ref):
    return [
        (slice(p, p + PAIR), h) for p in range(0, ref.shape[1], PAIR) for h in range(2)
    ]


def folded(combine, block):
    parts = [block[:, i : i + 128] for i in range(0, block.shape[1], 128)]
    while len(parts) > 1:
        parts = [combine(parts[i], parts[i + 1]) for i in range(0, len(parts), 2)]
    return parts[0]


def attend_kernel(first, lo, hi, q_ref, k_ref, v_ref, ql_ref, kl_ref, o_ref, lse_ref, s_ref, m_ref, l_ref, a_ref):
    block = pl.program_id(1)
    apart = apart_of()
    ql = ql_ref[...]
    heads = heads_of(q_ref)
    q = [own_head(q_ref[:, cols], h) for cols, h in heads]
    m_ref[...] = jnp.full(m_ref.shape, NEG, f32)
    l_ref[...] = jnp.zeros(l_ref.shape, f32)
    a_ref[...] = jnp.zeros(a_ref.shape, f32)

    def scores(kb, step, size):
        rows = block_rows(kb, size)
        seen = (ql == kl_ref[:, rows]) | (apart[:, :size] == (first + block - kb) * BLK)
        for i, (cols, _) in enumerate(heads):
            s = jnp.where(seen, against(q[i], k_ref[rows, cols]), NEG)
            s_ref[i, step, :, :size] = s
            m_ref[i] = jnp.maximum(m_ref[i], folded(jnp.maximum, s))

    over_range(scores, lo, hi, block)
    peaks = [jnp.max(m_ref[i], axis=1, keepdims=True) for i in range(len(heads))]

    def values(kb, step, size):
        rows = block_rows(kb, size)
        for i, (cols, _) in enumerate(heads):
            p = jnp.exp(s_ref[i, step, :, :size] - peaks[i])
            l_ref[i] = l_ref[i] + folded(jnp.add, p)
            a_ref[i] = a_ref[i] + product(p.astype(bf16), v_ref[rows, cols])

    over_range(values, lo, hi, block)
    totals = [jnp.sum(l_ref[i], axis=1, keepdims=True) for i in range(len(heads))]
    first_head = head_lanes(0)
    for i in range(0, len(heads), 2):
        cols = heads[i][0]
        o_ref[:, cols] = jnp.where(first_head, a_ref[i] / totals[i], a_ref[i + 1] / totals[i + 1])
        lse_ref[:, cols] = jnp.where(
            first_head, peaks[i] + jnp.log(totals[i]), peaks[i + 1] + jnp.log(totals[i + 1])
        )


def query_kernel(first, lo, hi, q_ref, k_ref, v_ref, ql_ref, kl_ref, do_ref, lse_ref, o_ref, dq_ref, a_ref):
    block = pl.program_id(1)
    apart = apart_of()
    ql = ql_ref[...]
    heads = heads_of(q_ref)
    q = [own_head(q_ref[:, cols], h) for cols, h in heads]
    do = [own_head(do_ref[:, cols], h) for cols, h in heads]
    lse = [lse_ref[:, i * HEAD_DIM : i * HEAD_DIM + 1] for i in range(len(heads))]
    delta = [
        jnp.sum(own_head(do_ref[:, cols].astype(f32) * o_ref[:, cols], h), axis=1, keepdims=True)
        for cols, h in heads
    ]
    a_ref[...] = jnp.zeros(a_ref.shape, f32)

    def take(kb, step, size):
        rows = block_rows(kb, size)
        seen = (ql == kl_ref[:, rows]) | (apart[:, :size] == (first + block - kb) * BLK)
        for i, (cols, _) in enumerate(heads):
            k = k_ref[rows, cols]
            p = jnp.exp(jnp.where(seen, against(q[i], k), NEG) - lse[i])
            ds = (p * (against(do[i], v_ref[rows, cols]) - delta[i])).astype(bf16)
            a_ref[i] = a_ref[i] + product(ds, k)

    over_range(take, lo, hi, block)
    for i in range(0, len(heads), 2):
        both = jnp.where(head_lanes(0), a_ref[i], a_ref[i + 1])
        dq_ref[:, heads[i][0]] = (both * (HEAD_DIM**-0.5)).astype(bf16)


def key_kernel(
    first, count, lo, hi, q_ref, k_ref, v_ref, ql_ref, kl_ref, g0, g1, g2, g3, g4, st_ref, dk_ref, dv_ref, a_ref, b_ref, do_ref
):
    block = pl.program_id(1)

    @pl.when(block == 0)
    def _():
        rows = q_ref.shape[0] // 8
        at = 0
        for ref in (g0, g1, g2, g3, g4):
            for c in range(ref.shape[0] // (rows + count)):
                do_ref[at : at + rows, :] = ref[c * (rows + count) : c * (rows + count) + rows, :]
                at += rows

    apart = apart_of()
    kl = kl_ref[...]
    heads = heads_of(k_ref)
    k = [own_head(k_ref[:, cols], h) for cols, h in heads]
    v = [own_head(v_ref[:, cols], h) for cols, h in heads]
    a_ref[...] = jnp.zeros(a_ref.shape, f32)
    b_ref[...] = jnp.zeros(b_ref.shape, f32)

    def take(qb, step, size):
        rows = block_rows(qb, size)
        seen = (kl == ql_ref[:, rows]) | (apart[:, :size] == (first + block - qb) * BLK)
        for i, (cols, h) in enumerate(heads):
            q = q_ref[rows, cols]
            do = do_ref[rows, cols]
            at = 2 * (i - h) + h
            p = jnp.exp(jnp.where(seen, against(k[i], q), NEG) - st_ref[at : at + 1, rows])
            ds = (p * (against(v[i], do) - st_ref[at + 2 : at + 3, rows])).astype(bf16)
            a_ref[i] = a_ref[i] + product(ds, q)
            b_ref[i] = b_ref[i] + product(p.astype(bf16), do)

    over_range(take, lo, hi, block)
    for i in range(0, len(heads), 2):
        cols = heads[i][0]
        dk_ref[:, cols] = jnp.where(head_lanes(0), a_ref[i], a_ref[i + 1]).astype(bf16)
        dv_ref[:, cols] = jnp.where(head_lanes(0), b_ref[i], b_ref[i + 1]).astype(bf16)


def dense_kernel(n_ref, gd_ref, wh_ref, wp_ref, bh_ref, act_ref, gh_ref, dw_ref, dbh_ref):
    n = n_ref[...]
    gd = gd_ref[...]
    for u in range(0, wh_ref.shape[2], BLK):
        units = slice(u, u + BLK)
        hidden = product(n, wh_ref[0, :, units]) + bh_ref[0, :, units]
        grad = against(gd, wp_ref[0, units, :])
        below = 0.5 + 0.5 * lax.erf(hidden * 0.7071067811865476)
        act = (hidden * below).astype(bf16)
        gh = grad * (below + hidden * (jnp.exp(-0.5 * hidden * hidden) * 0.3989422804014327))
        gh_low = gh.astype(bf16)
        act_ref[:, units] = act
        gh_ref[:, units] = gh_low
        dbh_ref[0, :, units] = jnp.sum(gh_low.astype(f32), axis=0, keepdims=True)
        dw_ref[1, 0, units, :] = inner_rows(act, gd).astype(bf16)
        dw_ref[0, 0, :, units] = inner_rows(n, gh_low).astype(bf16)


def dense_sum_kernel(act_ref, gh_ref, wh_ref, wp_ref, out_ref, gn_ref):
    @pl.when(pl.program_id(0) == 0)
    def _():
        out_ref[...] = jnp.zeros(out_ref.shape, f32)
        gn_ref[...] = jnp.zeros(gn_ref.shape, f32)

    out_ref[...] += product(act_ref[...], wp_ref[0])
    gn_ref[...] += against(gh_ref[...], wh_ref[0])


def dense_call(n, gd, weights, bias):
    rows, width = n.shape
    parts = weights.shape[0] // 2
    whole = pl.BlockSpec((rows, width), lambda j: (0, 0))
    columns = pl.BlockSpec((rows, width), lambda j: (0, j))
    chunk = pl.BlockSpec((1, width, width), lambda j: (j, 0, 0))
    second = pl.BlockSpec((1, width, width), lambda j: (parts + j, 0, 0))
    row = pl.BlockSpec((1, 1, width), lambda j: (j, 0, 0))
    params = pltpu.CompilerParams(vmem_limit_bytes=56 * 1024 * 1024)
    act, gh, dw, dbh = pl.pallas_call(
        dense_kernel,
        grid=(parts,),
        in_specs=[whole, whole, chunk, second, row],
        out_specs=[columns, columns, pl.BlockSpec((2, 1, width, width), lambda j: (0, j, 0, 0)), row],
        out_shape=[
            jax.ShapeDtypeStruct((rows, parts * width), bf16),
            jax.ShapeDtypeStruct((rows, parts * width), bf16),
            jax.ShapeDtypeStruct((2, parts, width, width), bf16),
            jax.ShapeDtypeStruct((parts, 1, width), f32),
        ],
        compiler_params=params,
        cost_estimate=pl.CostEstimate(flops=35_000_000_000, bytes_accessed=40_000_000, transcendentals=0),
    )(n, gd, weights, weights, bias)
    out, gn = pl.pallas_call(
        dense_sum_kernel,
        grid=(parts,),
        in_specs=[columns, columns, chunk, second],
        out_specs=[whole, whole],
        out_shape=[jax.ShapeDtypeStruct((rows, width), f32)] * 2,
        compiler_params=params,
        cost_estimate=pl.CostEstimate(flops=15_000_000_000, bytes_accessed=25_000_000, transcendentals=0),
    )(act, gh, weights, weights)
    return out, gn, dw.reshape(2 * parts, width, width), dbh


def attention_call(kernel, grid, in_specs, out_specs, out_shape, scratch, flops):
    return pl.pallas_call(
        kernel,
        grid_spec=pltpu.PrefetchScalarGridSpec(
            num_scalar_prefetch=2,
            grid=grid,
            in_specs=in_specs,
            out_specs=out_specs,
            scratch_shapes=scratch,
        ),
        out_shape=out_shape,
        compiler_params=pltpu.CompilerParams(vmem_limit_bytes=48 * 1024 * 1024),
        cost_estimate=pl.CostEstimate(flops=flops, bytes_accessed=8_000_000, transcendentals=0),
    )


def own_bit(bit):
    return (lax.axis_index("dev") >> bit) & 1


def swap(block, bit):
    count = lax.axis_size("dev")
    return lax.ppermute(block, "dev", [(i, i ^ (1 << bit)) for i in range(count)])


def shifted(block, distance):
    count = lax.axis_size("dev")
    return lax.ppermute(block, "dev", [(i, i + distance) for i in range(count) if 0 <= i + distance < count])


def pick(block, axis, index):
    return lax.dynamic_index_in_dim(block, index, axis, keepdims=False)


def halves(blocks, bits, bit, kind=bf16):
    axis = bits.index(bit)
    mine = own_bit(bit)
    sent = jnp.concatenate([pick(b, axis, 1 - mine) for b in blocks], axis=-2).astype(kind)
    kept = jnp.concatenate([pick(b, axis, mine) for b in blocks], axis=-2)
    return kept, swap(sent, bit)


def added(kept, arrived):
    return (kept.astype(f32) + arrived.astype(f32)).astype(arrived.dtype)


class Travelling:
    def __init__(self, block, bits, order, kind=bf16):
        self.block, self.bits, self.order, self.kind = block, list(bits), list(order), kind

    def send(self):
        bit = self.order.pop(0)
        self.kept, self.arriving = halves([self.block], self.bits, bit, self.kind)
        self.bits.remove(bit)

    def receive(self, *beside):
        return received([self], *beside)


def received(travellers, *beside):
    tied = lax.optimization_barrier((*[t.arriving for t in travellers], *beside))
    for part, arrived in zip(travellers, tied):
        part.block = added(part.kept, arrived)
    return tied[len(travellers) :]


def on_device(
    tokens,
    cotangent,
    segment_ids,
    validity,
    first_gain,
    first_bias,
    query_weight,
    query_bias,
    key_weight,
    value_weight,
    value_bias,
    output_weight,
    output_bias,
    attention_scale,
    second_gain,
    second_bias,
    hidden_weight,
    hidden_bias,
    project_weight,
    project_bias,
    dense_scale,
):
    count = lax.axis_size("dev")
    depth = count.bit_length() - 1
    rows, width = tokens.shape
    half = width // 2
    window = 8 * rows
    assert 1 << depth == count and 2 * rows + rows >= IMG - 1 and rows % BLK == 0
    core = own_bit(0)
    shard = query_weight.shape[0]
    ff = hidden_weight.shape[1]
    parts = ff // width

    vectors = jnp.concatenate(
        [
            v.reshape(-1, shard).T
            for v in (
                first_gain,
                first_bias,
                query_bias,
                value_bias,
                output_bias,
                attention_scale,
                second_gain,
                second_bias,
                project_bias,
                dense_scale,
                hidden_bias,
            )
        ],
        axis=1,
    )
    vectors = jnp.pad(vectors, ((0, 0), (0, 128 - vectors.shape[1])))
    attention_pack = jnp.concatenate(
        [w[:, c * half : (c + 1) * half] for c in range(2) for w in (query_weight, key_weight, value_weight)]
        + [output_weight, vectors],
        axis=1,
    )
    hidden_local = hidden_weight.reshape(shard, count, parts, shard).transpose(2, 0, 1, 3).reshape(parts, shard, width)
    dense_pack = jnp.concatenate([hidden_local, project_weight.reshape(parts, shard, width)])
    attention_full = lax.all_gather(attention_pack, "dev", axis=0, tiled=True)
    dense_full = lax.all_gather(dense_pack, "dev", axis=1, tiled=True)

    labels = segment_ids + 1
    tag_rows = jnp.stack(
        [jnp.concatenate([labels % 256, labels // 256]), jnp.concatenate([validity, jnp.zeros_like(validity)])]
    ).astype(bf16)
    tag_rows = jnp.pad(tag_rows, ((0, 14), (0, 0)))
    own = jnp.concatenate([tokens, tag_rows])
    below = shifted(own, 2)
    above = shifted(own, -2)
    far = lax.ppermute(
        own,
        "dev",
        [(i, i - 4) for i in range(4, count, 2)] + [(i, i + 4) for i in range(1, count - 4, 2)],
    )
    mine = jnp.stack([below, own, above, far])
    theirs = swap(mine, 0)
    zero, one = jnp.where(core == 0, mine, theirs), jnp.where(core == 0, theirs, mine)
    blocks = [one[3], zero[0], one[0], zero[1], one[1], zero[2], one[2], zero[3]]
    window_tokens = jnp.concatenate([b[:rows] for b in blocks])
    tags = jnp.stack([b[rows : rows + 2] for b in blocks]).astype(jnp.int32)
    window_labels = (tags[:, 0, :rows] + 256 * tags[:, 0, rows:]).reshape(window)
    window_valid = tags[:, 1, :rows].reshape(window)
    key_label = jnp.where(window_valid == 1, window_labels, 0)
    query_label = jnp.where(window_labels == 0, -1, window_labels)
    first_row, last_row = 3 * rows, 5 * rows
    own_blocks = 2 * rows // BLK
    index = lax.broadcasted_iota(jnp.int32, (own_blocks, window), 1)
    block_labels = window_labels[first_row:last_row].reshape(own_blocks, BLK)
    lo = jnp.min(jnp.where(window_labels[None] == block_labels[:, :1], index, window), axis=1) // BLK
    hi = jnp.max(jnp.where(window_labels[None] == block_labels[:, -1:], index, -1), axis=1) // BLK + 1

    columns = attention_full[:, 4 * width :].T.astype(f32)
    (
        gain_first,
        bias_first,
        bias_query,
        bias_value,
        bias_output,
        scale_first,
        gain_second,
        bias_second,
        bias_project,
        scale_second,
    ) = [columns[i] for i in range(10)]
    bias_hidden = columns[10 : 10 + parts].reshape(parts, 1, width)
    weight_qkv = lax.dynamic_slice_in_dim(attention_full, core * 3 * half, 3 * half, 1)
    weight_output = attention_full[:, 3 * width : 4 * width]

    normed_window = layer_norm(window_tokens.astype(f32), gain_first, bias_first).astype(bf16)
    start = core * half
    bias_qkv = jnp.concatenate(
        [
            lax.dynamic_slice_in_dim(bias_query, start, half),
            jnp.zeros((half,), f32),
            lax.dynamic_slice_in_dim(bias_value, start, half),
        ]
    )
    scale_qkv = jnp.concatenate([jnp.full((half,), HEAD_DIM**-0.5, f32), jnp.ones((2 * half,), f32)])
    projected = ((product(normed_window, weight_qkv) + bias_qkv) * scale_qkv).astype(bf16)

    pairs = half // PAIR
    first = first_row // BLK

    def own_rows(group, lanes=half):
        return pl.BlockSpec((BLK, lanes), lambda h, b, lo, hi: (first + b, group * (half // lanes) + h))

    def all_rows(group, lanes=half):
        return pl.BlockSpec((window, lanes), lambda h, b, lo, hi: (0, group * (half // lanes) + h))

    row_block = pl.BlockSpec((BLK, half), lambda h, b, lo, hi: (b, 0))
    label_rows = pl.BlockSpec((BLK, 1), lambda h, b, lo, hi: (first + b, 0))
    label_all = pl.BlockSpec((1, window), lambda h, b, lo, hi: (0, 0))
    lanes = half // 2
    heads = lanes // HEAD_DIM
    half_block = pl.BlockSpec((BLK, lanes), lambda h, b, lo, hi: (b, h))
    attended_f, lse = attention_call(
        partial(attend_kernel, first),
        (half // lanes, own_blocks),
        [own_rows(0, lanes), all_rows(1, lanes), all_rows(2, lanes), label_rows, label_all],
        [half_block, half_block],
        [jax.ShapeDtypeStruct((2 * rows, half), f32)] * 2,
        [pltpu.VMEM((heads, window // STEP, BLK, STEP), f32)] + [pltpu.VMEM((heads, BLK, PAIR), f32)] * 3,
        50_000_000_000,
    )(lo, hi, projected, projected, projected, query_label[:, None], key_label[None])

    def columns_of(c, mine, theirs):
        return jnp.where(c == 0, jnp.concatenate([mine, theirs], 1), jnp.concatenate([theirs, mine], 1))

    attended_half = attended_f.astype(bf16)
    one_column = (jnp.arange(2 * pairs)[:, None] * HEAD_DIM == jnp.arange(half)[None]).astype(f32)
    lse_rows = lax.dot_general(one_column, lse, (((1,), (1,)), ((), ())), precision=lax.Precision.HIGHEST)
    attended_low = columns_of(
        core,
        lax.dynamic_slice_in_dim(attended_half, core * rows, rows, 0),
        swap(lax.dynamic_slice_in_dim(attended_half, (1 - core) * rows, rows, 0), 0),
    )
    inputs = tokens.astype(f32)
    branch = product(attended_low, weight_output) + bias_output
    middle = inputs + scale_first * branch

    normed_two, second_norm_back = jax.vjp(layer_norm, middle, gain_second, bias_second)
    upstream = cotangent.astype(f32)
    grad_dense = (upstream * scale_second).astype(bf16)
    chip_tokens = window_tokens[first_row:last_row].astype(f32)
    chip_center = chip_tokens - jnp.mean(chip_tokens, axis=-1, keepdims=True)
    chip_inverse = lax.rsqrt(jnp.mean(chip_center * chip_center, axis=-1, keepdims=True) + norm_eps)
    chip_unit = chip_center * chip_inverse
    normed_two_low, lse_rows, chip_unit, chip_inverse = lax.optimization_barrier(
        (normed_two.astype(bf16), lse_rows, chip_unit, chip_inverse)
    )
    dense_sum, grad_normed_two, dense_weight_grads, hidden_bias_grad = dense_call(
        normed_two_low, grad_dense, dense_full, bias_hidden
    )
    project_bias_grad = column_sums(grad_dense)
    grad_middle_norm, second_gain_grad, second_bias_grad = second_norm_back(grad_normed_two)
    grad_middle = upstream + grad_middle_norm
    grad_branch = (grad_middle * scale_first).astype(bf16)
    grad_attended = against(grad_branch, weight_output).astype(bf16)

    dense_sums = lax.psum_scatter(dense_weight_grads, "dev", scatter_dimension=1, tiled=True)
    bits = list(range(depth - 1, -1, -1))
    chips = bits[:-1][::-1]
    axes, far_bits = chips[:3], chips[3:]

    output_weight_grad = inner_rows(attended_low, grad_branch).astype(bf16)
    output_kept, output_other = halves([output_weight_grad.reshape((2,) * depth + (shard, width))], bits, 0)

    grad_half = jnp.where(core == 0, grad_attended[:, :half], grad_attended[:, half:])
    grad_other = swap(jnp.where(core == 0, grad_attended[:, half:], grad_attended[:, :half]), 0)
    grad_pair = jnp.where(
        core == 0, jnp.concatenate([grad_half, grad_other]), jnp.concatenate([grad_other, grad_half])
    )
    member = (jnp.arange(2 * pairs)[:, None] == jnp.arange(half)[None] // HEAD_DIM).astype(f32)
    delta = lax.dot_general(
        member, grad_pair.astype(f32) * attended_f, (((1,), (1,)), ((), ())), precision=lax.Precision.HIGHEST
    )
    stats = jnp.stack([lse_rows.reshape(pairs, 2, -1), delta.reshape(pairs, 2, -1)], axis=1).reshape(4 * pairs, -1)
    top = lax.reduce_precision(stats, 8, 7)
    mid = lax.reduce_precision(stats - top, 8, 7)
    pieces = jnp.concatenate([top, mid, stats - top - mid]).astype(bf16)
    stat_count = pieces.shape[0]
    packed = [jnp.concatenate([grad_pair[c * rows : (c + 1) * rows], pieces[:, c * rows : (c + 1) * rows]]) for c in range(2)]
    both = jnp.concatenate(packed)
    from_below = shifted(both, 2)
    from_above = shifted(both, -2)
    far_below = shifted(packed[1], 4)
    far_above = shifted(packed[0], -4)
    (grad_queries,) = attention_call(
        partial(query_kernel, first),
        (1, own_blocks),
        [own_rows(0), all_rows(1), all_rows(2), label_rows, label_all, row_block, row_block, row_block],
        [row_block],
        [jax.ShapeDtypeStruct((2 * rows, half), bf16)],
        [pltpu.VMEM((2 * pairs, BLK, PAIR), f32)],
        60_000_000_000,
    )(lo, hi, projected, projected, projected, query_label[:, None], key_label[None], grad_pair, lse, attended_f)
    from_below, from_above, far_below, far_above, output_other, grad_queries = lax.optimization_barrier(
        (from_below, from_above, far_below, far_above, output_other, grad_queries)
    )
    normed_pair = normed_window[first_row:last_row]
    chip_view = (2,) * (depth - 1) + (2 * shard, half)

    def weight_sum(grad):
        return inner_rows(normed_pair, grad).astype(bf16).reshape(chip_view)

    output_chip = added(output_kept, output_other)
    output_chip = jnp.concatenate([output_chip[..., :half], output_chip[..., half:]], axis=-2)
    first_part = Travelling(
        jnp.concatenate([weight_sum(grad_queries), output_chip], axis=-1),
        bits[:-1],
        [axes[2]] + far_bits + [axes[0], axes[1]],
    )
    first_part.send()
    unit = rows + stat_count
    own_unit = both
    stat_parts = [far_below[rows:]]
    for piece in (from_below, own_unit, from_above):
        stat_parts += [piece[rows:unit], piece[unit + rows :]]
    stat_parts.append(far_above[rows:])
    stat_window = jnp.concatenate(stat_parts, axis=1).astype(f32)
    third = 4 * pairs
    stat_window = stat_window[:third] + stat_window[third : 2 * third] + stat_window[2 * third :]
    one_unit = pl.BlockSpec((unit, half), lambda h, b, lo, hi: (0, 0))
    two_units = pl.BlockSpec((2 * unit, half), lambda h, b, lo, hi: (0, 0))
    grad_keys, grad_values = attention_call(
        partial(key_kernel, first, stat_count),
        (1, own_blocks),
        [
            all_rows(0),
            own_rows(1),
            own_rows(2),
            label_all,
            label_rows,
            one_unit,
            two_units,
            two_units,
            two_units,
            one_unit,
            pl.BlockSpec((4 * pairs, window), lambda h, b, lo, hi: (0, 0)),
        ],
        [row_block, row_block],
        [jax.ShapeDtypeStruct((2 * rows, half), bf16)] * 2,
        [pltpu.VMEM((2 * pairs, BLK, PAIR), f32)] * 2 + [pltpu.VMEM((window, half), bf16)],
        70_000_000_000,
    )(lo, hi, projected, projected, projected, query_label[None], key_label[:, None], far_below, from_below, own_unit, from_above, far_above, stat_window)

    grad_keys, grad_values, grad_branch, grad_middle, dense_sum = first_part.receive(
        grad_keys, grad_values, grad_branch, grad_middle, dense_sum
    )
    key_part = Travelling(weight_sum(grad_keys), bits[:-1], [axes[0], axes[1], axes[2]] + far_bits)
    value_part = Travelling(weight_sum(grad_values), bits[:-1], [axes[1], axes[2], axes[0]] + far_bits)
    for part in (key_part, value_part, first_part):
        part.send()
    grad_all = jnp.concatenate([grad_queries, grad_keys, grad_values], axis=1)
    grad_normed_pair = against(grad_all, weight_qkv)
    grad_normed_own = lax.dynamic_slice_in_dim(grad_normed_pair, core * rows, rows, 0)
    grad_normed_other = swap(lax.dynamic_slice_in_dim(grad_normed_pair, (1 - core) * rows, rows, 0), 0)
    first_gain_grad = jnp.sum(grad_normed_pair * chip_unit, axis=0)
    first_bias_grad = jnp.sum(grad_normed_pair, axis=0)
    output_bias_grad = column_sums(grad_branch)
    attention_scale_grad = jnp.sum(grad_middle * branch, axis=0)
    dense_out = dense_sum + bias_project
    layer_output = (middle + scale_second * dense_out).astype(bf16)
    dense_scale_grad = jnp.sum(upstream * dense_out, axis=0)

    def placed_half(values):
        spread = jnp.zeros((width,), f32)
        return lax.dynamic_update_slice_in_dim(spread, values, core * half, 0)

    grads = [
        first_gain_grad,
        first_bias_grad,
        placed_half(column_sums(grad_queries)),
        placed_half(column_sums(grad_values)),
        output_bias_grad,
        attention_scale_grad,
        second_gain_grad,
        second_bias_grad,
        project_bias_grad,
        dense_scale_grad,
        hidden_bias_grad.reshape(parts, count, shard).transpose(1, 0, 2),
    ]
    vector_rows = jnp.concatenate([g.reshape(count, -1) for g in grads], axis=1)
    vector_rows = jnp.pad(vector_rows, ((0, 0), (0, -vector_rows.shape[1] % 128)))
    vector_part = Travelling(vector_rows.reshape((2,) * depth + (1, -1)), bits, bits[::-1], f32)
    vector_part.send()
    grad_normed_own, grad_normed_other, layer_output = received(
        (key_part, value_part, first_part, vector_part), grad_normed_own, grad_normed_other, layer_output
    )
    for part in (key_part, value_part, first_part, vector_part):
        part.send()

    grad_normed = grad_normed_own + grad_normed_other
    unit_rows = lax.dynamic_slice_in_dim(chip_unit, core * rows, rows, 0)
    inverse = lax.dynamic_slice_in_dim(chip_inverse, core * rows, rows, 0)
    gained = grad_normed * gain_first
    along = jnp.mean(gained * unit_rows, axis=-1, keepdims=True)
    gained = gained - jnp.mean(gained, axis=-1, keepdims=True) - unit_rows * along
    input_gradient = grad_middle + gained * inverse

    moving = [key_part, value_part, first_part, vector_part]
    swapped = {}

    def to_core(name, part):
        kept = lax.dynamic_slice_in_dim(part.block, core * shard, shard, 0)
        sent = lax.dynamic_slice_in_dim(part.block, (1 - core) * shard, shard, 0)
        if name == "first":
            swapped["output"] = part.block[:, half:]
            kept, sent = kept[:, :half], sent[:, :half]
        swapped[name] = (kept, swap(sent, 0))

    names = {id(key_part): "key", id(value_part): "value", id(first_part): "first"}
    turn = 0
    while moving:
        if turn == 0:
            input_gradient, dense_sums = received(moving, input_gradient, dense_sums)
            project_out = dense_sums[parts:].reshape(parts * shard, width).astype(f32)
            hidden_out = dense_sums[:parts].reshape(parts, shard, count, shard)
            hidden_out = hidden_out.transpose(1, 2, 0, 3).reshape(shard, ff).astype(f32)
        elif turn == 1:
            project_out, hidden_out = received(moving, project_out, hidden_out)
        else:
            received(moving)
        still = []
        for part in moving:
            if part.order:
                part.send()
                still.append(part)
            elif id(part) in names:
                to_core(names[id(part)], part)
        moving = still
        turn += 1
    query_out, key_out, value_out = [columns_of(core, *swapped[n]).astype(f32) for n in ("first", "key", "value")]
    output_out = jnp.concatenate([swapped["output"][:shard], swapped["output"][shard:]], axis=1).astype(f32)
    vector_sum = vector_part.block[0]
    out = [vector_sum[i * shard : (i + 1) * shard] for i in range(10)]
    hidden_bias_out = vector_sum[10 * shard : (10 + parts) * shard]
    return (
        layer_output,
        input_gradient,
        out[0],
        out[1],
        query_out,
        out[2],
        key_out,
        value_out,
        out[3],
        output_out,
        out[4],
        out[5],
        out[6],
        out[7],
        hidden_out,
        hidden_bias_out,
        project_out,
        out[8],
        out[9],
    )


def solution(mesh):
    placed = (
        P("dev", None),
        P("dev", None),
        P("dev"),
        P("dev"),
        P("dev"),
        P("dev"),
        P("dev", None),
        P("dev"),
        P("dev", None),
        P("dev", None),
        P("dev"),
        P("dev", None),
        P("dev"),
        P("dev"),
        P("dev"),
        P("dev"),
        P("dev", None),
        P("dev"),
        P("dev", None),
        P("dev"),
        P("dev"),
    )
    return jax.shard_map(
        on_device,
        mesh=mesh,
        in_specs=placed,
        out_specs=(
            P("dev", None),
            P("dev", None),
            P("dev"),
            P("dev"),
            P("dev", None),
            P("dev"),
            P("dev", None),
            P("dev", None),
            P("dev"),
            P("dev", None),
            P("dev"),
            P("dev"),
            P("dev"),
            P("dev"),
            P("dev", None),
            P("dev"),
            P("dev", None),
            P("dev"),
            P("dev"),
        ),
        check_vma=False,
    )
```

```python
from functools import partial
import jax
import jax.numpy as jnp
from jax import lax
from jax.experimental import pallas as pl
from jax.experimental.pallas import tpu as pltpu
from jax.sharding import PartitionSpec as P

HEAD_DIM = 64
PAIR = 2 * HEAD_DIM
IMG = 1370
BLK = 256
STEP = 512
norm_eps = 1e-06
bf16 = jnp.bfloat16
f32 = jnp.float32
NEG = -1e30


def layer_norm(row_values, gain_row, bias_row):
    center = row_values - jnp.mean(row_values, axis=-1, keepdims=True)
    spread = jnp.mean(center * center, axis=-1, keepdims=True)
    return center * lax.rsqrt(spread + norm_eps) * gain_row + bias_row


def product(a, b):
    return jnp.dot(a, b, preferred_element_type=f32)


def inner_rows(a, b):
    return lax.dot_general(a, b, (((0,), (0,)), ((), ())), preferred_element_type=f32)


def against(a, b):
    return lax.dot_general(a, b, (((1,), (1,)), ((), ())), preferred_element_type=f32)


def column_sums(rows):
    return jnp.sum(rows.astype(f32), axis=0)


def head_lanes(h):
    lane = lax.broadcasted_iota(jnp.int32, (1, PAIR), 1)
    return (lane >= h * HEAD_DIM) & (lane < (h + 1) * HEAD_DIM)


def own_head(block, h):
    return jnp.where(head_lanes(h), block, jnp.zeros_like(block))


def over_range(body, lo, hi, block):
    per = STEP // BLK
    start, count = lo[block], hi[block] - lo[block]
    steps = count // per

    def take(step, carried):
        body(start + per * step, step, STEP)
        return carried

    lax.fori_loop(0, steps, take, 0)

    @pl.when(count % per > 0)
    def _():
        body(start + per * steps, steps, BLK)


def apart_of():
    shape = (BLK, STEP)
    return lax.broadcasted_iota(jnp.int32, shape, 1) - lax.broadcasted_iota(jnp.int32, shape, 0)


def block_rows(block, size):
    return pl.ds(pl.multiple_of(block * BLK, BLK), size)


def heads_of(ref):
    return [
        (slice(p, p + PAIR), h) for p in range(0, ref.shape[1], PAIR) for h in range(2)
    ]


def folded(combine, block):
    parts = [block[:, i : i + 128] for i in range(0, block.shape[1], 128)]
    while len(parts) > 1:
        parts = [combine(parts[i], parts[i + 1]) for i in range(0, len(parts), 2)]
    return parts[0]


def attend_kernel(first, lo, hi, q_ref, k_ref, v_ref, ql_ref, kl_ref, o_ref, lse_ref, s_ref, m_ref, l_ref, a_ref):
    block = pl.program_id(1)
    apart = apart_of()
    ql = ql_ref[...]
    heads = heads_of(q_ref)
    q = [own_head(q_ref[:, cols], h) for cols, h in heads]
    m_ref[...] = jnp.full(m_ref.shape, NEG, f32)
    l_ref[...] = jnp.zeros(l_ref.shape, f32)
    a_ref[...] = jnp.zeros(a_ref.shape, f32)

    def scores(kb, step, size):
        rows = block_rows(kb, size)
        seen = (ql == kl_ref[:, rows]) | (apart[:, :size] == (first + block - kb) * BLK)
        for i, (cols, _) in enumerate(heads):
            s = jnp.where(seen, against(q[i], k_ref[rows, cols]), NEG)
            s_ref[i, step, :, :size] = s
            m_ref[i] = jnp.maximum(m_ref[i], folded(jnp.maximum, s))

    over_range(scores, lo, hi, block)
    peaks = [jnp.max(m_ref[i], axis=1, keepdims=True) for i in range(len(heads))]

    def values(kb, step, size):
        rows = block_rows(kb, size)
        for i, (cols, _) in enumerate(heads):
            p = jnp.exp(s_ref[i, step, :, :size] - peaks[i])
            l_ref[i] = l_ref[i] + folded(jnp.add, p)
            a_ref[i] = a_ref[i] + product(p.astype(bf16), v_ref[rows, cols])

    over_range(values, lo, hi, block)
    totals = [jnp.sum(l_ref[i], axis=1, keepdims=True) for i in range(len(heads))]
    first_head = head_lanes(0)
    for i in range(0, len(heads), 2):
        cols = heads[i][0]
        o_ref[:, cols] = jnp.where(first_head, a_ref[i] / totals[i], a_ref[i + 1] / totals[i + 1])
        lse_ref[:, cols] = jnp.where(
            first_head, peaks[i] + jnp.log(totals[i]), peaks[i + 1] + jnp.log(totals[i + 1])
        )


def query_kernel(first, lo, hi, q_ref, k_ref, v_ref, ql_ref, kl_ref, do_ref, lse_ref, o_ref, dq_ref, a_ref):
    block = pl.program_id(1)
    apart = apart_of()
    ql = ql_ref[...]
    heads = heads_of(q_ref)
    q = [own_head(q_ref[:, cols], h) for cols, h in heads]
    do = [own_head(do_ref[:, cols], h) for cols, h in heads]
    lse = [lse_ref[:, i * HEAD_DIM : i * HEAD_DIM + 1] for i in range(len(heads))]
    delta = [
        jnp.sum(own_head(do_ref[:, cols].astype(f32) * o_ref[:, cols], h), axis=1, keepdims=True)
        for cols, h in heads
    ]
    a_ref[...] = jnp.zeros(a_ref.shape, f32)

    def take(kb, step, size):
        rows = block_rows(kb, size)
        seen = (ql == kl_ref[:, rows]) | (apart[:, :size] == (first + block - kb) * BLK)
        for i, (cols, _) in enumerate(heads):
            k = k_ref[rows, cols]
            p = jnp.exp(jnp.where(seen, against(q[i], k), NEG) - lse[i])
            ds = (p * (against(do[i], v_ref[rows, cols]) - delta[i])).astype(bf16)
            a_ref[i] = a_ref[i] + product(ds, k)

    over_range(take, lo, hi, block)
    for i in range(0, len(heads), 2):
        both = jnp.where(head_lanes(0), a_ref[i], a_ref[i + 1])
        dq_ref[:, heads[i][0]] = (both * (HEAD_DIM**-0.5)).astype(bf16)


def key_kernel(
    first, count, lo, hi, q_ref, k_ref, v_ref, ql_ref, kl_ref, g0, g1, g2, g3, g4, st_ref, dk_ref, dv_ref, a_ref, b_ref, do_ref
):
    block = pl.program_id(1)

    @pl.when(block == 0)
    def _():
        rows = q_ref.shape[0] // 8
        far = g0.shape[0] - count
        left_out = jnp.zeros((rows - far, q_ref.shape[1]), bf16)
        do_ref[: rows - far, :] = left_out
        do_ref[rows - far : rows, :] = g0[:far, :]
        at = rows
        for ref in (g1, g2, g3):
            for c in range(2):
                do_ref[at : at + rows, :] = ref[c * (rows + count) : c * (rows + count) + rows, :]
                at += rows
        do_ref[at : at + far, :] = g4[:far, :]
        do_ref[at + far :, :] = left_out

    apart = apart_of()
    kl = kl_ref[...]
    heads = heads_of(k_ref)
    k = [own_head(k_ref[:, cols], h) for cols, h in heads]
    v = [own_head(v_ref[:, cols], h) for cols, h in heads]
    a_ref[...] = jnp.zeros(a_ref.shape, f32)
    b_ref[...] = jnp.zeros(b_ref.shape, f32)

    def take(qb, step, size):
        rows = block_rows(qb, size)
        seen = (kl == ql_ref[:, rows]) | (apart[:, :size] == (first + block - qb) * BLK)
        for i, (cols, h) in enumerate(heads):
            q = q_ref[rows, cols]
            do = do_ref[rows, cols]
            at = 2 * (i - h) + h
            p = jnp.exp(jnp.where(seen, against(k[i], q), NEG) - st_ref[at : at + 1, rows])
            ds = (p * (against(v[i], do) - st_ref[at + 2 : at + 3, rows])).astype(bf16)
            a_ref[i] = a_ref[i] + product(ds, q)
            b_ref[i] = b_ref[i] + product(p.astype(bf16), do)

    over_range(take, lo, hi, block)
    for i in range(0, len(heads), 2):
        cols = heads[i][0]
        dk_ref[:, cols] = jnp.where(head_lanes(0), a_ref[i], a_ref[i + 1]).astype(bf16)
        dv_ref[:, cols] = jnp.where(head_lanes(0), b_ref[i], b_ref[i + 1]).astype(bf16)


def dense_kernel(n_ref, gd_ref, wh_ref, wp_ref, bh_ref, act_ref, gh_ref, dw_ref, dbh_ref):
    n = n_ref[...]
    gd = gd_ref[...]
    for u in range(0, wh_ref.shape[2], STEP):
        units = slice(u, u + STEP)
        hidden = product(n, wh_ref[0, :, units]) + bh_ref[0, :, units]
        grad = against(gd, wp_ref[0, units, :])
        below = 0.5 + 0.5 * lax.erf(hidden * 0.7071067811865476)
        act = (hidden * below).astype(bf16)
        gh = grad * (below + hidden * (jnp.exp(-0.5 * hidden * hidden) * 0.3989422804014327))
        gh_low = gh.astype(bf16)
        act_ref[:, units] = act
        gh_ref[:, units] = gh_low
        dbh_ref[0, :, units] = jnp.sum(gh_low.astype(f32), axis=0, keepdims=True)
        dw_ref[1, 0, units, :] = inner_rows(act, gd).astype(bf16)
        dw_ref[0, 0, :, units] = inner_rows(n, gh_low).astype(bf16)


def forward_sum_kernel(act_ref, wp_ref, out_ref):
    @pl.when(pl.program_id(0) == 0)
    def _():
        out_ref[...] = jnp.zeros(out_ref.shape, f32)

    out_ref[...] += product(act_ref[...], wp_ref[0])


def backward_sum_kernel(gh_ref, wh_ref, gn_ref):
    @pl.when(pl.program_id(0) == 0)
    def _():
        gn_ref[...] = jnp.zeros(gn_ref.shape, f32)

    gn_ref[...] += against(gh_ref[...], wh_ref[0])


def sum_call(kernel, units, weights, at):
    rows, width = units.shape[0], weights.shape[2]
    return pl.pallas_call(
        kernel,
        grid=(units.shape[1] // width,),
        in_specs=[
            pl.BlockSpec((rows, width), lambda j: (0, j)),
            pl.BlockSpec((1, width, width), lambda j: (at + j, 0, 0)),
        ],
        out_specs=pl.BlockSpec((rows, width), lambda j: (0, 0)),
        out_shape=jax.ShapeDtypeStruct((rows, width), f32),
        compiler_params=pltpu.CompilerParams(vmem_limit_bytes=40 * 1024 * 1024),
        cost_estimate=pl.CostEstimate(flops=8_000_000_000, bytes_accessed=12_000_000, transcendentals=0),
    )(units, weights)


def dense_call(n, gd, weights, bias):
    rows, width = n.shape
    parts = weights.shape[0] // 2
    whole = pl.BlockSpec((rows, width), lambda j: (0, 0))
    columns = pl.BlockSpec((rows, width), lambda j: (0, j))
    chunk = pl.BlockSpec((1, width, width), lambda j: (j, 0, 0))
    second = pl.BlockSpec((1, width, width), lambda j: (parts + j, 0, 0))
    row = pl.BlockSpec((1, 1, width), lambda j: (j, 0, 0))
    params = pltpu.CompilerParams(vmem_limit_bytes=56 * 1024 * 1024)
    act, gh, dw, dbh = pl.pallas_call(
        dense_kernel,
        grid=(parts,),
        in_specs=[whole, whole, chunk, second, row],
        out_specs=[columns, columns, pl.BlockSpec((2, 1, width, width), lambda j: (0, j, 0, 0)), row],
        out_shape=[
            jax.ShapeDtypeStruct((rows, parts * width), bf16),
            jax.ShapeDtypeStruct((rows, parts * width), bf16),
            jax.ShapeDtypeStruct((2, parts, width, width), bf16),
            jax.ShapeDtypeStruct((parts, 1, width), f32),
        ],
        compiler_params=params,
        cost_estimate=pl.CostEstimate(flops=35_000_000_000, bytes_accessed=40_000_000, transcendentals=0),
    )(n, gd, weights, weights, bias)
    return act, sum_call(backward_sum_kernel, gh, weights, 0), dw.reshape(2 * parts, width, width), dbh


def attention_call(kernel, grid, in_specs, out_specs, out_shape, scratch, flops):
    return pl.pallas_call(
        kernel,
        grid_spec=pltpu.PrefetchScalarGridSpec(
            num_scalar_prefetch=2,
            grid=grid,
            in_specs=in_specs,
            out_specs=out_specs,
            scratch_shapes=scratch,
        ),
        out_shape=out_shape,
        compiler_params=pltpu.CompilerParams(vmem_limit_bytes=48 * 1024 * 1024),
        cost_estimate=pl.CostEstimate(flops=flops, bytes_accessed=8_000_000, transcendentals=0),
    )


def own_bit(bit):
    return (lax.axis_index("dev") >> bit) & 1


def swap(block, bit):
    count = lax.axis_size("dev")
    return lax.ppermute(block, "dev", [(i, i ^ (1 << bit)) for i in range(count)])


def shifted(block, distance):
    count = lax.axis_size("dev")
    return lax.ppermute(block, "dev", [(i, i + distance) for i in range(count) if 0 <= i + distance < count])


def pick(block, axis, index):
    return lax.dynamic_index_in_dim(block, index, axis, keepdims=False)


def halves(blocks, bits, bit, kind=bf16):
    axis = bits.index(bit)
    mine = own_bit(bit)
    sent = jnp.concatenate([pick(b, axis, 1 - mine) for b in blocks], axis=-2).astype(kind)
    kept = jnp.concatenate([pick(b, axis, mine) for b in blocks], axis=-2)
    return kept, swap(sent, bit)


def added(kept, arrived):
    return (kept.astype(f32) + arrived.astype(f32)).astype(arrived.dtype)


class Travelling:
    def __init__(self, block, bits, order, kind=bf16):
        self.block, self.bits, self.order, self.kind = block, list(bits), list(order), kind

    def send(self):
        bit = self.order.pop(0)
        self.kept, self.arriving = halves([self.block], self.bits, bit, self.kind)
        self.bits.remove(bit)

    def receive(self, *beside):
        return received([self], *beside)


def received(travellers, *beside):
    tied = lax.optimization_barrier((*[t.arriving for t in travellers], *beside))
    for part, arrived in zip(travellers, tied):
        part.block = added(part.kept, arrived)
    return tied[len(travellers) :]


def on_device(
    tokens,
    cotangent,
    segment_ids,
    validity,
    first_gain,
    first_bias,
    query_weight,
    query_bias,
    key_weight,
    value_weight,
    value_bias,
    output_weight,
    output_bias,
    attention_scale,
    second_gain,
    second_bias,
    hidden_weight,
    hidden_bias,
    project_weight,
    project_bias,
    dense_scale,
):
    count = lax.axis_size("dev")
    depth = count.bit_length() - 1
    rows, width = tokens.shape
    half = width // 2
    window = 8 * rows
    assert 1 << depth == count and 2 * rows + rows >= IMG - 1 and rows % BLK == 0
    core = own_bit(0)
    shard = query_weight.shape[0]
    ff = hidden_weight.shape[1]
    parts = ff // width

    vectors = jnp.concatenate(
        [
            v.reshape(-1, shard).T
            for v in (
                first_gain,
                first_bias,
                query_bias,
                value_bias,
                output_bias,
                attention_scale,
                second_gain,
                second_bias,
                project_bias,
                dense_scale,
                hidden_bias,
            )
        ],
        axis=1,
    )
    vectors = jnp.pad(vectors, ((0, 0), (0, 128 - vectors.shape[1])))
    attention_pack = jnp.concatenate(
        [w[:, c * half : (c + 1) * half] for c in range(2) for w in (query_weight, key_weight, value_weight)]
        + [output_weight, vectors],
        axis=1,
    )
    hidden_local = hidden_weight.reshape(shard, count, parts, shard).transpose(2, 0, 1, 3).reshape(parts, shard, width)
    dense_pack = jnp.concatenate([hidden_local, project_weight.reshape(parts, shard, width)])
    attention_full = lax.all_gather(attention_pack, "dev", axis=0, tiled=True)
    dense_full = lax.all_gather(dense_pack, "dev", axis=1, tiled=True)

    labels = segment_ids + 1
    tag_rows = jnp.stack(
        [jnp.concatenate([labels % 256, labels // 256]), jnp.concatenate([validity, jnp.zeros_like(validity)])]
    ).astype(bf16)
    tag_rows = jnp.pad(tag_rows, ((0, 14), (0, 0)))
    own = jnp.concatenate([tokens, tag_rows])
    below = shifted(own, 2)
    above = shifted(own, -2)
    far_rows = -(-(IMG - 1 - 2 * rows) // 16) * 16
    left_out = jnp.zeros((rows - far_rows, width), bf16)
    far = lax.ppermute(
        jnp.concatenate([jnp.where(core == 0, tokens[:far_rows], tokens[rows - far_rows :]), tag_rows]),
        "dev",
        [(i, i - 4) for i in range(4, count, 2)] + [(i, i + 4) for i in range(1, count - 4, 2)],
    )
    far = jnp.where(
        core == 0,
        jnp.concatenate([far[:far_rows], left_out, far[far_rows:]]),
        jnp.concatenate([left_out, far]),
    )
    mine = jnp.stack([below, own, above, far])
    theirs = swap(mine, 0)
    zero, one = jnp.where(core == 0, mine, theirs), jnp.where(core == 0, theirs, mine)
    blocks = [one[3], zero[0], one[0], zero[1], one[1], zero[2], one[2], zero[3]]
    window_tokens = jnp.concatenate([b[:rows] for b in blocks])
    tags = jnp.stack([b[rows : rows + 2] for b in blocks]).astype(jnp.int32)
    window_labels = (tags[:, 0, :rows] + 256 * tags[:, 0, rows:]).reshape(window)
    window_valid = tags[:, 1, :rows].reshape(window)
    key_label = jnp.where(window_valid == 1, window_labels, 0)
    query_label = jnp.where(window_labels == 0, -1, window_labels)
    first_row, last_row = 3 * rows, 5 * rows
    own_blocks = 2 * rows // BLK
    index = lax.broadcasted_iota(jnp.int32, (own_blocks, window), 1)
    block_labels = window_labels[first_row:last_row].reshape(own_blocks, BLK)
    lo = jnp.min(jnp.where(window_labels[None] == block_labels[:, :1], index, window), axis=1) // BLK
    hi = jnp.max(jnp.where(window_labels[None] == block_labels[:, -1:], index, -1), axis=1) // BLK + 1

    columns = attention_full[:, 4 * width :].T.astype(f32)
    (
        gain_first,
        bias_first,
        bias_query,
        bias_value,
        bias_output,
        scale_first,
        gain_second,
        bias_second,
        bias_project,
        scale_second,
    ) = [columns[i] for i in range(10)]
    bias_hidden = columns[10 : 10 + parts].reshape(parts, 1, width)
    weight_qkv = lax.dynamic_slice_in_dim(attention_full, core * 3 * half, 3 * half, 1)
    weight_output = attention_full[:, 3 * width : 4 * width]

    normed_window = layer_norm(window_tokens.astype(f32), gain_first, bias_first).astype(bf16)
    start = core * half
    bias_qkv = jnp.concatenate(
        [
            lax.dynamic_slice_in_dim(bias_query, start, half),
            jnp.zeros((half,), f32),
            lax.dynamic_slice_in_dim(bias_value, start, half),
        ]
    )
    scale_qkv = jnp.concatenate([jnp.full((half,), HEAD_DIM**-0.5, f32), jnp.ones((2 * half,), f32)])
    projected = ((product(normed_window, weight_qkv) + bias_qkv) * scale_qkv).astype(bf16)

    pairs = half // PAIR
    first = first_row // BLK

    def own_rows(group, lanes=half):
        return pl.BlockSpec((BLK, lanes), lambda h, b, lo, hi: (first + b, group * (half // lanes) + h))

    def all_rows(group, lanes=half):
        return pl.BlockSpec((window, lanes), lambda h, b, lo, hi: (0, group * (half // lanes) + h))

    row_block = pl.BlockSpec((BLK, half), lambda h, b, lo, hi: (b, 0))
    label_rows = pl.BlockSpec((BLK, 1), lambda h, b, lo, hi: (first + b, 0))
    label_all = pl.BlockSpec((1, window), lambda h, b, lo, hi: (0, 0))
    lanes = half // 2
    heads = lanes // HEAD_DIM
    half_block = pl.BlockSpec((BLK, lanes), lambda h, b, lo, hi: (b, h))
    attended_f, lse = attention_call(
        partial(attend_kernel, first),
        (half // lanes, own_blocks),
        [own_rows(0, lanes), all_rows(1, lanes), all_rows(2, lanes), label_rows, label_all],
        [half_block, half_block],
        [jax.ShapeDtypeStruct((2 * rows, half), f32)] * 2,
        [pltpu.VMEM((heads, window // STEP, BLK, STEP), f32)] + [pltpu.VMEM((heads, BLK, PAIR), f32)] * 3,
        50_000_000_000,
    )(lo, hi, projected, projected, projected, query_label[:, None], key_label[None])

    def columns_of(c, mine, theirs):
        return jnp.where(c == 0, jnp.concatenate([mine, theirs], 1), jnp.concatenate([theirs, mine], 1))

    attended_half = attended_f.astype(bf16)
    one_column = (jnp.arange(2 * pairs)[:, None] * HEAD_DIM == jnp.arange(half)[None]).astype(f32)
    lse_rows = lax.dot_general(one_column, lse, (((1,), (1,)), ((), ())), precision=lax.Precision.HIGHEST)
    attended_low = columns_of(
        core,
        lax.dynamic_slice_in_dim(attended_half, core * rows, rows, 0),
        swap(lax.dynamic_slice_in_dim(attended_half, (1 - core) * rows, rows, 0), 0),
    )
    inputs = tokens.astype(f32)
    branch = product(attended_low, weight_output) + bias_output
    middle = inputs + scale_first * branch

    normed_two, second_norm_back = jax.vjp(layer_norm, middle, gain_second, bias_second)
    upstream = cotangent.astype(f32)
    grad_dense = (upstream * scale_second).astype(bf16)
    chip_tokens = window_tokens[first_row:last_row].astype(f32)
    chip_center = chip_tokens - jnp.mean(chip_tokens, axis=-1, keepdims=True)
    chip_inverse = lax.rsqrt(jnp.mean(chip_center * chip_center, axis=-1, keepdims=True) + norm_eps)
    chip_unit = chip_center * chip_inverse
    normed_two_low, lse_rows, chip_unit, chip_inverse = lax.optimization_barrier(
        (normed_two.astype(bf16), lse_rows, chip_unit, chip_inverse)
    )
    active, grad_normed_two, dense_weight_grads, hidden_bias_grad = dense_call(
        normed_two_low, grad_dense, dense_full, bias_hidden
    )
    project_bias_grad = column_sums(grad_dense)
    grad_middle_norm, second_gain_grad, second_bias_grad = second_norm_back(grad_normed_two)
    grad_middle = upstream + grad_middle_norm
    grad_branch = (grad_middle * scale_first).astype(bf16)
    grad_attended = against(grad_branch, weight_output).astype(bf16)

    dense_sums = lax.psum_scatter(dense_weight_grads, "dev", scatter_dimension=1, tiled=True)
    bits = list(range(depth - 1, -1, -1))
    chips = bits[:-1][::-1]
    axes, far_bits = chips[:3], chips[3:]

    output_weight_grad = inner_rows(attended_low, grad_branch).astype(bf16)
    output_kept, output_other = halves([output_weight_grad.reshape((2,) * depth + (shard, width))], bits, 0)

    grad_half = jnp.where(core == 0, grad_attended[:, :half], grad_attended[:, half:])
    grad_other = swap(jnp.where(core == 0, grad_attended[:, half:], grad_attended[:, :half]), 0)
    grad_pair = jnp.where(
        core == 0, jnp.concatenate([grad_half, grad_other]), jnp.concatenate([grad_other, grad_half])
    )
    member = (jnp.arange(2 * pairs)[:, None] == jnp.arange(half)[None] // HEAD_DIM).astype(f32)
    delta = lax.dot_general(
        member, grad_pair.astype(f32) * attended_f, (((1,), (1,)), ((), ())), precision=lax.Precision.HIGHEST
    )
    stats = jnp.stack([lse_rows.reshape(pairs, 2, -1), delta.reshape(pairs, 2, -1)], axis=1).reshape(4 * pairs, -1)
    top = lax.reduce_precision(stats, 8, 7)
    mid = lax.reduce_precision(stats - top, 8, 7)
    pieces = jnp.concatenate([top, mid, stats - top - mid]).astype(bf16)
    stat_count = pieces.shape[0]
    packed = [jnp.concatenate([grad_pair[c * rows : (c + 1) * rows], pieces[:, c * rows : (c + 1) * rows]]) for c in range(2)]
    both = jnp.concatenate(packed)
    from_below = shifted(both, 2)
    from_above = shifted(both, -2)
    far_below = shifted(packed[1][rows - far_rows :], 4)
    far_above = shifted(jnp.concatenate([packed[0][:far_rows], packed[0][rows:]]), -4)
    (grad_queries,) = attention_call(
        partial(query_kernel, first),
        (1, own_blocks),
        [own_rows(0), all_rows(1), all_rows(2), label_rows, label_all, row_block, row_block, row_block],
        [row_block],
        [jax.ShapeDtypeStruct((2 * rows, half), bf16)],
        [pltpu.VMEM((2 * pairs, BLK, PAIR), f32)],
        60_000_000_000,
    )(lo, hi, projected, projected, projected, query_label[:, None], key_label[None], grad_pair, lse, attended_f)
    from_below, from_above, far_below, far_above, output_other, grad_queries = lax.optimization_barrier(
        (from_below, from_above, far_below, far_above, output_other, grad_queries)
    )
    normed_pair = normed_window[first_row:last_row]
    chip_view = (2,) * (depth - 1) + (2 * shard, half)

    def weight_sum(grad):
        return inner_rows(normed_pair, grad).astype(bf16).reshape(chip_view)

    output_chip = added(output_kept, output_other)
    output_chip = jnp.concatenate([output_chip[..., :half], output_chip[..., half:]], axis=-2)
    first_part = Travelling(
        jnp.concatenate([weight_sum(grad_queries), output_chip], axis=-1),
        bits[:-1],
        [axes[2]] + far_bits + [axes[0], axes[1]],
    )
    first_part.send()
    unit = rows + stat_count
    own_unit = both
    stat_parts = [far_below[far_rows:]]
    for piece in (from_below, own_unit, from_above):
        stat_parts += [piece[rows:unit], piece[unit + rows :]]
    stat_parts.append(far_above[far_rows:])
    stat_window = jnp.concatenate(stat_parts, axis=1).astype(f32)
    third = 4 * pairs
    stat_window = stat_window[:third] + stat_window[third : 2 * third] + stat_window[2 * third :]
    one_unit = pl.BlockSpec((far_rows + stat_count, half), lambda h, b, lo, hi: (0, 0))
    two_units = pl.BlockSpec((2 * unit, half), lambda h, b, lo, hi: (0, 0))
    grad_keys, grad_values = attention_call(
        partial(key_kernel, first, stat_count),
        (1, own_blocks),
        [
            all_rows(0),
            own_rows(1),
            own_rows(2),
            label_all,
            label_rows,
            one_unit,
            two_units,
            two_units,
            two_units,
            one_unit,
            pl.BlockSpec((4 * pairs, window), lambda h, b, lo, hi: (0, 0)),
        ],
        [row_block, row_block],
        [jax.ShapeDtypeStruct((2 * rows, half), bf16)] * 2,
        [pltpu.VMEM((2 * pairs, BLK, PAIR), f32)] * 2 + [pltpu.VMEM((window, half), bf16)],
        70_000_000_000,
    )(lo, hi, projected, projected, projected, query_label[None], key_label[:, None], far_below, from_below, own_unit, from_above, far_above, stat_window)

    grad_keys, grad_values, grad_branch, grad_middle, active = first_part.receive(
        grad_keys, grad_values, grad_branch, grad_middle, active
    )
    key_part = Travelling(weight_sum(grad_keys), bits[:-1], [axes[0], axes[1], axes[2]] + far_bits)
    value_part = Travelling(weight_sum(grad_values), bits[:-1], [axes[1], axes[2], axes[0]] + far_bits)
    for part in (key_part, value_part, first_part):
        part.send()
    grad_all = jnp.concatenate([grad_queries, grad_keys, grad_values], axis=1)
    grad_normed_pair = against(grad_all, weight_qkv)
    grad_normed_own = lax.dynamic_slice_in_dim(grad_normed_pair, core * rows, rows, 0)
    grad_normed_other = swap(lax.dynamic_slice_in_dim(grad_normed_pair, (1 - core) * rows, rows, 0), 0)
    first_gain_grad = jnp.sum(grad_normed_pair * chip_unit, axis=0)
    first_bias_grad = jnp.sum(grad_normed_pair, axis=0)
    output_bias_grad = column_sums(grad_branch)
    attention_scale_grad = jnp.sum(grad_middle * branch, axis=0)
    dense_out = sum_call(forward_sum_kernel, active, dense_full, parts) + bias_project
    layer_output = (middle + scale_second * dense_out).astype(bf16)
    dense_scale_grad = jnp.sum(upstream * dense_out, axis=0)

    def placed_half(values):
        spread = jnp.zeros((width,), f32)
        return lax.dynamic_update_slice_in_dim(spread, values, core * half, 0)

    grads = [
        first_gain_grad,
        first_bias_grad,
        placed_half(column_sums(grad_queries)),
        placed_half(column_sums(grad_values)),
        output_bias_grad,
        attention_scale_grad,
        second_gain_grad,
        second_bias_grad,
        project_bias_grad,
        dense_scale_grad,
        hidden_bias_grad.reshape(parts, count, shard).transpose(1, 0, 2),
    ]
    vector_rows = jnp.concatenate([g.reshape(count, -1) for g in grads], axis=1)
    vector_rows = jnp.pad(vector_rows, ((0, 0), (0, -vector_rows.shape[1] % 128)))
    vector_part = Travelling(vector_rows.reshape((2,) * depth + (1, -1)), bits, bits[::-1], f32)
    vector_part.send()
    grad_normed_own, grad_normed_other, layer_output = received(
        (key_part, value_part, first_part, vector_part), grad_normed_own, grad_normed_other, layer_output
    )
    for part in (key_part, value_part, first_part, vector_part):
        part.send()

    grad_normed = grad_normed_own + grad_normed_other
    unit_rows = lax.dynamic_slice_in_dim(chip_unit, core * rows, rows, 0)
    inverse = lax.dynamic_slice_in_dim(chip_inverse, core * rows, rows, 0)
    gained = grad_normed * gain_first
    along = jnp.mean(gained * unit_rows, axis=-1, keepdims=True)
    gained = gained - jnp.mean(gained, axis=-1, keepdims=True) - unit_rows * along
    input_gradient = grad_middle + gained * inverse

    moving = [key_part, value_part, first_part, vector_part]
    swapped = {}

    def to_core(name, part):
        kept = lax.dynamic_slice_in_dim(part.block, core * shard, shard, 0)
        sent = lax.dynamic_slice_in_dim(part.block, (1 - core) * shard, shard, 0)
        if name == "first":
            swapped["output"] = part.block[:, half:]
            kept, sent = kept[:, :half], sent[:, :half]
        swapped[name] = (kept, swap(sent, 0))

    names = {id(key_part): "key", id(value_part): "value", id(first_part): "first"}
    turn = 0
    while moving:
        if turn == 0:
            input_gradient, dense_sums = received(moving, input_gradient, dense_sums)
            project_out = dense_sums[parts:].reshape(parts * shard, width).astype(f32)
            hidden_out = dense_sums[:parts].reshape(parts, shard, count, shard)
            hidden_out = hidden_out.transpose(1, 2, 0, 3).reshape(shard, ff).astype(f32)
        elif turn == 1:
            project_out, hidden_out = received(moving, project_out, hidden_out)
        else:
            received(moving)
        still = []
        for part in moving:
            if part.order:
                part.send()
                still.append(part)
            elif id(part) in names:
                to_core(names[id(part)], part)
        moving = still
        turn += 1
    query_out, key_out, value_out = [columns_of(core, *swapped[n]).astype(f32) for n in ("first", "key", "value")]
    output_out = jnp.concatenate([swapped["output"][:shard], swapped["output"][shard:]], axis=1).astype(f32)
    vector_sum = vector_part.block[0]
    out = [vector_sum[i * shard : (i + 1) * shard] for i in range(10)]
    hidden_bias_out = vector_sum[10 * shard : (10 + parts) * shard]
    return (
        layer_output,
        input_gradient,
        out[0],
        out[1],
        query_out,
        out[2],
        key_out,
        value_out,
        out[3],
        output_out,
        out[4],
        out[5],
        out[6],
        out[7],
        hidden_out,
        hidden_bias_out,
        project_out,
        out[8],
        out[9],
    )


def solution(mesh):
    placed = (
        P("dev", None),
        P("dev", None),
        P("dev"),
        P("dev"),
        P("dev"),
        P("dev"),
        P("dev", None),
        P("dev"),
        P("dev", None),
        P("dev", None),
        P("dev"),
        P("dev", None),
        P("dev"),
        P("dev"),
        P("dev"),
        P("dev"),
        P("dev", None),
        P("dev"),
        P("dev", None),
        P("dev"),
        P("dev"),
    )
    return jax.shard_map(
        on_device,
        mesh=mesh,
        in_specs=placed,
        out_specs=(
            P("dev", None),
            P("dev", None),
            P("dev"),
            P("dev"),
            P("dev", None),
            P("dev"),
            P("dev", None),
            P("dev", None),
            P("dev"),
            P("dev", None),
            P("dev"),
            P("dev"),
            P("dev"),
            P("dev"),
            P("dev", None),
            P("dev"),
            P("dev", None),
            P("dev"),
            P("dev"),
        ),
        check_vma=False,
    )
```

```python
from functools import partial
import jax
import jax.numpy as jnp
from jax import lax
from jax.experimental import pallas as pl
from jax.experimental.pallas import tpu as pltpu
from jax.sharding import PartitionSpec as P

HEAD_DIM = 64
PAIR = 2 * HEAD_DIM
IMG = 1370
BLK = 256
STEP = 512
norm_eps = 1e-06
bf16 = jnp.bfloat16
f32 = jnp.float32
NEG = -1e30


def layer_norm(row_values, gain_row, bias_row):
    center = row_values - jnp.mean(row_values, axis=-1, keepdims=True)
    spread = jnp.mean(center * center, axis=-1, keepdims=True)
    return center * lax.rsqrt(spread + norm_eps) * gain_row + bias_row


def product(a, b):
    return jnp.dot(a, b, preferred_element_type=f32)


def inner_rows(a, b):
    return lax.dot_general(a, b, (((0,), (0,)), ((), ())), preferred_element_type=f32)


def against(a, b):
    return lax.dot_general(a, b, (((1,), (1,)), ((), ())), preferred_element_type=f32)


def column_sums(rows):
    return jnp.sum(rows.astype(f32), axis=0)


def head_lanes(h):
    lane = lax.broadcasted_iota(jnp.int32, (1, PAIR), 1)
    return (lane >= h * HEAD_DIM) & (lane < (h + 1) * HEAD_DIM)


def own_head(block, h):
    return jnp.where(head_lanes(h), block, jnp.zeros_like(block))


def over_range(body, lo, hi, block):
    per = STEP // BLK
    start, count = lo[block], hi[block] - lo[block]
    steps = count // per

    def take(step, carried):
        body(start + per * step, step, STEP)
        return carried

    lax.fori_loop(0, steps, take, 0)

    @pl.when(count % per > 0)
    def _():
        body(start + per * steps, steps, BLK)


def apart_of():
    shape = (BLK, STEP)
    return lax.broadcasted_iota(jnp.int32, shape, 1) - lax.broadcasted_iota(jnp.int32, shape, 0)


def block_rows(block, size):
    return pl.ds(pl.multiple_of(block * BLK, BLK), size)


def heads_of(ref):
    return [
        (slice(p, p + PAIR), h) for p in range(0, ref.shape[1], PAIR) for h in range(2)
    ]


def folded(combine, block):
    parts = [block[:, i : i + 128] for i in range(0, block.shape[1], 128)]
    while len(parts) > 1:
        parts = [combine(parts[i], parts[i + 1]) for i in range(0, len(parts), 2)]
    return parts[0]


def attend_kernel(first, lo, hi, q_ref, k_ref, v_ref, ql_ref, kl_ref, o_ref, lse_ref, s_ref, m_ref, l_ref, a_ref):
    block = pl.program_id(1)
    apart = apart_of()
    ql = ql_ref[...]
    heads = heads_of(q_ref)
    q = [own_head(q_ref[:, cols], h) for cols, h in heads]
    m_ref[...] = jnp.full(m_ref.shape, NEG, f32)
    l_ref[...] = jnp.zeros(l_ref.shape, f32)
    a_ref[...] = jnp.zeros(a_ref.shape, f32)

    def scores(kb, step, size):
        rows = block_rows(kb, size)
        seen = (ql == kl_ref[:, rows]) | (apart[:, :size] == (first + block - kb) * BLK)
        for i, (cols, _) in enumerate(heads):
            s = jnp.where(seen, against(q[i], k_ref[rows, cols]), NEG)
            s_ref[i, step, :, :size] = s
            m_ref[i] = jnp.maximum(m_ref[i], folded(jnp.maximum, s))

    over_range(scores, lo, hi, block)
    peaks = [jnp.max(m_ref[i], axis=1, keepdims=True) for i in range(len(heads))]

    def values(kb, step, size):
        rows = block_rows(kb, size)
        for i, (cols, _) in enumerate(heads):
            p = jnp.exp(s_ref[i, step, :, :size] - peaks[i])
            l_ref[i] = l_ref[i] + folded(jnp.add, p)
            a_ref[i] = a_ref[i] + product(p.astype(bf16), v_ref[rows, cols])

    over_range(values, lo, hi, block)
    totals = [jnp.sum(l_ref[i], axis=1, keepdims=True) for i in range(len(heads))]
    first_head = head_lanes(0)
    for i in range(0, len(heads), 2):
        cols = heads[i][0]
        o_ref[:, cols] = jnp.where(first_head, a_ref[i] / totals[i], a_ref[i + 1] / totals[i + 1])
        lse_ref[:, cols] = jnp.where(
            first_head, peaks[i] + jnp.log(totals[i]), peaks[i + 1] + jnp.log(totals[i + 1])
        )


def query_kernel(first, lo, hi, q_ref, k_ref, v_ref, ql_ref, kl_ref, do_ref, lse_ref, o_ref, dq_ref, a_ref):
    block = pl.program_id(1)
    apart = apart_of()
    ql = ql_ref[...]
    heads = heads_of(q_ref)
    q = [own_head(q_ref[:, cols], h) for cols, h in heads]
    do = [own_head(do_ref[:, cols], h) for cols, h in heads]
    lse = [lse_ref[:, i * HEAD_DIM : i * HEAD_DIM + 1] for i in range(len(heads))]
    delta = [
        jnp.sum(own_head(do_ref[:, cols].astype(f32) * o_ref[:, cols], h), axis=1, keepdims=True)
        for cols, h in heads
    ]
    a_ref[...] = jnp.zeros(a_ref.shape, f32)

    def take(kb, step, size):
        rows = block_rows(kb, size)
        seen = (ql == kl_ref[:, rows]) | (apart[:, :size] == (first + block - kb) * BLK)
        for i, (cols, _) in enumerate(heads):
            k = k_ref[rows, cols]
            p = jnp.exp(jnp.where(seen, against(q[i], k), NEG) - lse[i])
            ds = (p * (against(do[i], v_ref[rows, cols]) - delta[i])).astype(bf16)
            a_ref[i] = a_ref[i] + product(ds, k)

    over_range(take, lo, hi, block)
    for i in range(0, len(heads), 2):
        both = jnp.where(head_lanes(0), a_ref[i], a_ref[i + 1])
        dq_ref[:, heads[i][0]] = (both * (HEAD_DIM**-0.5)).astype(bf16)


def key_kernel(
    first, count, lo, hi, q_ref, k_ref, v_ref, ql_ref, kl_ref, g0, g1, g2, g3, g4, st_ref, dk_ref, dv_ref, a_ref, b_ref, do_ref
):
    block = pl.program_id(1)

    @pl.when(block == 0)
    def _():
        rows = q_ref.shape[0] // 8
        far = g0.shape[0] - count
        left_out = jnp.zeros((rows - far, q_ref.shape[1]), bf16)
        do_ref[: rows - far, :] = left_out
        do_ref[rows - far : rows, :] = g0[:far, :]
        at = rows
        for ref in (g1, g2, g3):
            for c in range(2):
                do_ref[at : at + rows, :] = ref[c * (rows + count) : c * (rows + count) + rows, :]
                at += rows
        do_ref[at : at + far, :] = g4[:far, :]
        do_ref[at + far :, :] = left_out

    apart = apart_of()
    kl = kl_ref[...]
    heads = heads_of(k_ref)
    k = [own_head(k_ref[:, cols], h) for cols, h in heads]
    v = [own_head(v_ref[:, cols], h) for cols, h in heads]
    a_ref[...] = jnp.zeros(a_ref.shape, f32)
    b_ref[...] = jnp.zeros(b_ref.shape, f32)

    def take(qb, step, size):
        rows = block_rows(qb, size)
        seen = (kl == ql_ref[:, rows]) | (apart[:, :size] == (first + block - qb) * BLK)
        for i, (cols, h) in enumerate(heads):
            q = q_ref[rows, cols]
            do = do_ref[rows, cols]
            at = 2 * (i - h) + h
            p = jnp.exp(jnp.where(seen, against(k[i], q), NEG) - st_ref[at : at + 1, rows])
            ds = (p * (against(v[i], do) - st_ref[at + 2 : at + 3, rows])).astype(bf16)
            a_ref[i] = a_ref[i] + product(ds, q)
            b_ref[i] = b_ref[i] + product(p.astype(bf16), do)

    over_range(take, lo, hi, block)
    for i in range(0, len(heads), 2):
        cols = heads[i][0]
        dk_ref[:, cols] = jnp.where(head_lanes(0), a_ref[i], a_ref[i + 1]).astype(bf16)
        dv_ref[:, cols] = jnp.where(head_lanes(0), b_ref[i], b_ref[i + 1]).astype(bf16)


def dense_kernel(n_ref, gd_ref, wh_ref, wp_ref, bh_ref, act_ref, gh_ref, dw_ref, dbh_ref):
    n = n_ref[...]
    gd = gd_ref[...]
    for u in range(0, wh_ref.shape[2], STEP):
        units = slice(u, u + STEP)
        hidden = product(n, wh_ref[0, :, units]) + bh_ref[0, :, units]
        grad = against(gd, wp_ref[0, units, :])
        below = 0.5 + 0.5 * lax.erf(hidden * 0.7071067811865476)
        act = (hidden * below).astype(bf16)
        gh = grad * (below + hidden * (jnp.exp(-0.5 * hidden * hidden) * 0.3989422804014327))
        gh_low = gh.astype(bf16)
        act_ref[:, units] = act
        gh_ref[:, units] = gh_low
        dbh_ref[0, :, units] = jnp.sum(gh_low.astype(f32), axis=0, keepdims=True)
        dw_ref[1, 0, units, :] = inner_rows(act, gd).astype(bf16)
        dw_ref[0, 0, :, units] = inner_rows(n, gh_low).astype(bf16)


def forward_sum_kernel(act_ref, wp_ref, out_ref):
    @pl.when(pl.program_id(0) == 0)
    def _():
        out_ref[...] = jnp.zeros(out_ref.shape, f32)

    out_ref[...] += product(act_ref[...], wp_ref[0])


def backward_sum_kernel(gh_ref, wh_ref, gn_ref):
    @pl.when(pl.program_id(0) == 0)
    def _():
        gn_ref[...] = jnp.zeros(gn_ref.shape, f32)

    gn_ref[...] += against(gh_ref[...], wh_ref[0])


def sum_call(kernel, units, weights, at):
    rows, width = units.shape[0], weights.shape[2]
    return pl.pallas_call(
        kernel,
        grid=(units.shape[1] // width,),
        in_specs=[
            pl.BlockSpec((rows, width), lambda j: (0, j)),
            pl.BlockSpec((1, width, width), lambda j: (at + j, 0, 0)),
        ],
        out_specs=pl.BlockSpec((rows, width), lambda j: (0, 0)),
        out_shape=jax.ShapeDtypeStruct((rows, width), f32),
        compiler_params=pltpu.CompilerParams(vmem_limit_bytes=40 * 1024 * 1024),
        cost_estimate=pl.CostEstimate(flops=8_000_000_000, bytes_accessed=12_000_000, transcendentals=0),
    )(units, weights)


def dense_call(n, gd, weights, bias):
    rows, width = n.shape
    parts = weights.shape[0] // 2
    whole = pl.BlockSpec((rows, width), lambda j: (0, 0))
    columns = pl.BlockSpec((rows, width), lambda j: (0, j))
    chunk = pl.BlockSpec((1, width, width), lambda j: (j, 0, 0))
    second = pl.BlockSpec((1, width, width), lambda j: (parts + j, 0, 0))
    row = pl.BlockSpec((1, 1, width), lambda j: (j, 0, 0))
    params = pltpu.CompilerParams(vmem_limit_bytes=56 * 1024 * 1024)
    act, gh, dw, dbh = pl.pallas_call(
        dense_kernel,
        grid=(parts,),
        in_specs=[whole, whole, chunk, second, row],
        out_specs=[columns, columns, pl.BlockSpec((2, 1, width, width), lambda j: (0, j, 0, 0)), row],
        out_shape=[
            jax.ShapeDtypeStruct((rows, parts * width), bf16),
            jax.ShapeDtypeStruct((rows, parts * width), bf16),
            jax.ShapeDtypeStruct((2, parts, width, width), bf16),
            jax.ShapeDtypeStruct((parts, 1, width), f32),
        ],
        compiler_params=params,
        cost_estimate=pl.CostEstimate(flops=35_000_000_000, bytes_accessed=40_000_000, transcendentals=0),
    )(n, gd, weights, weights, bias)
    return act, sum_call(backward_sum_kernel, gh, weights, 0), dw.reshape(2 * parts, width, width), dbh


def ungroup_kernel(g_ref, out_ref):
    groups, rows, width = g_ref.shape
    share = 128 // groups
    lane = lax.broadcasted_iota(jnp.int32, (rows, 128), 1)
    for t in range(0, width, 128):
        tiles = [g_ref[j, :, t : t + 128].astype(f32) for j in range(groups)]
        for i in range(groups):
            tile = tiles[i]
            for j in range(groups):
                if j != i:
                    moved = pltpu.roll(tiles[j], (j - i) * share % 128, 1)
                    tile = jnp.where(lane // share == j, moved, tile)
            at = groups * t + 128 * i
            out_ref[:, at : at + 128] = tile


def attention_call(kernel, grid, in_specs, out_specs, out_shape, scratch, flops):
    return pl.pallas_call(
        kernel,
        grid_spec=pltpu.PrefetchScalarGridSpec(
            num_scalar_prefetch=2,
            grid=grid,
            in_specs=in_specs,
            out_specs=out_specs,
            scratch_shapes=scratch,
        ),
        out_shape=out_shape,
        compiler_params=pltpu.CompilerParams(vmem_limit_bytes=48 * 1024 * 1024),
        cost_estimate=pl.CostEstimate(flops=flops, bytes_accessed=8_000_000, transcendentals=0),
    )


def own_bit(bit):
    return (lax.axis_index("dev") >> bit) & 1


def swap(block, bit):
    count = lax.axis_size("dev")
    return lax.ppermute(block, "dev", [(i, i ^ (1 << bit)) for i in range(count)])


def shifted(block, distance):
    count = lax.axis_size("dev")
    return lax.ppermute(block, "dev", [(i, i + distance) for i in range(count) if 0 <= i + distance < count])


def pick(block, axis, index):
    return lax.dynamic_index_in_dim(block, index, axis, keepdims=False)


def halves(blocks, bits, bit, kind=bf16):
    axis = bits.index(bit)
    mine = own_bit(bit)
    sent = jnp.concatenate([pick(b, axis, 1 - mine) for b in blocks], axis=-2).astype(kind)
    kept = jnp.concatenate([pick(b, axis, mine) for b in blocks], axis=-2)
    return kept, swap(sent, bit)


def added(kept, arrived):
    return (kept.astype(f32) + arrived.astype(f32)).astype(arrived.dtype)


class Travelling:
    def __init__(self, block, bits, order, kind=bf16):
        self.block, self.bits, self.order, self.kind = block, list(bits), list(order), kind

    def send(self):
        bit = self.order.pop(0)
        self.kept, self.arriving = halves([self.block], self.bits, bit, self.kind)
        self.bits.remove(bit)

    def receive(self, *beside):
        return received([self], *beside)


def received(travellers, *beside):
    tied = lax.optimization_barrier((*[t.arriving for t in travellers], *beside))
    for part, arrived in zip(travellers, tied):
        part.block = added(part.kept, arrived)
    return tied[len(travellers) :]


def on_device(
    tokens,
    cotangent,
    segment_ids,
    validity,
    first_gain,
    first_bias,
    query_weight,
    query_bias,
    key_weight,
    value_weight,
    value_bias,
    output_weight,
    output_bias,
    attention_scale,
    second_gain,
    second_bias,
    hidden_weight,
    hidden_bias,
    project_weight,
    project_bias,
    dense_scale,
):
    count = lax.axis_size("dev")
    depth = count.bit_length() - 1
    rows, width = tokens.shape
    half = width // 2
    window = 8 * rows
    assert 1 << depth == count and 2 * rows + rows >= IMG - 1 and rows % BLK == 0
    core = own_bit(0)
    shard = query_weight.shape[0]
    ff = hidden_weight.shape[1]
    parts = ff // width

    vectors = jnp.concatenate(
        [
            v.reshape(-1, shard).T
            for v in (
                first_gain,
                first_bias,
                query_bias,
                value_bias,
                output_bias,
                attention_scale,
                second_gain,
                second_bias,
                project_bias,
                dense_scale,
                hidden_bias,
            )
        ],
        axis=1,
    )
    vectors = jnp.pad(vectors, ((0, 0), (0, 128 - vectors.shape[1])))
    attention_pack = jnp.concatenate(
        [w[:, c * half : (c + 1) * half] for c in range(2) for w in (query_weight, key_weight, value_weight)]
        + [output_weight, vectors],
        axis=1,
    )
    hidden_local = hidden_weight.reshape(shard, count, parts, shard).transpose(2, 0, 1, 3).reshape(parts, shard, width)
    dense_pack = jnp.concatenate([hidden_local, project_weight.reshape(parts, shard, width)])
    attention_full = lax.all_gather(attention_pack, "dev", axis=0, tiled=True)
    dense_full = lax.all_gather(dense_pack, "dev", axis=1, tiled=True)

    labels = segment_ids + 1
    tag_rows = jnp.stack(
        [jnp.concatenate([labels % 256, labels // 256]), jnp.concatenate([validity, jnp.zeros_like(validity)])]
    ).astype(bf16)
    tag_rows = jnp.pad(tag_rows, ((0, 14), (0, 0)))
    own = jnp.concatenate([tokens, tag_rows])
    below = shifted(own, 2)
    above = shifted(own, -2)
    far_rows = -(-(IMG - 1 - 2 * rows) // 16) * 16
    left_out = jnp.zeros((rows - far_rows, width), bf16)
    far = lax.ppermute(
        jnp.concatenate([jnp.where(core == 0, tokens[:far_rows], tokens[rows - far_rows :]), tag_rows]),
        "dev",
        [(i, i - 4) for i in range(4, count, 2)] + [(i, i + 4) for i in range(1, count - 4, 2)],
    )
    far = jnp.where(
        core == 0,
        jnp.concatenate([far[:far_rows], left_out, far[far_rows:]]),
        jnp.concatenate([left_out, far]),
    )
    mine = jnp.stack([below, own, above, far])
    theirs = swap(mine, 0)
    zero, one = jnp.where(core == 0, mine, theirs), jnp.where(core == 0, theirs, mine)
    blocks = [one[3], zero[0], one[0], zero[1], one[1], zero[2], one[2], zero[3]]
    window_tokens = jnp.concatenate([b[:rows] for b in blocks])
    tags = jnp.stack([b[rows : rows + 2] for b in blocks]).astype(jnp.int32)
    window_labels = (tags[:, 0, :rows] + 256 * tags[:, 0, rows:]).reshape(window)
    window_valid = tags[:, 1, :rows].reshape(window)
    key_label = jnp.where(window_valid == 1, window_labels, 0)
    query_label = jnp.where(window_labels == 0, -1, window_labels)
    first_row, last_row = 3 * rows, 5 * rows
    own_blocks = 2 * rows // BLK
    index = lax.broadcasted_iota(jnp.int32, (own_blocks, window), 1)
    block_labels = window_labels[first_row:last_row].reshape(own_blocks, BLK)
    lo = jnp.min(jnp.where(window_labels[None] == block_labels[:, :1], index, window), axis=1) // BLK
    hi = jnp.max(jnp.where(window_labels[None] == block_labels[:, -1:], index, -1), axis=1) // BLK + 1

    columns = attention_full[:, 4 * width :].T.astype(f32)
    (
        gain_first,
        bias_first,
        bias_query,
        bias_value,
        bias_output,
        scale_first,
        gain_second,
        bias_second,
        bias_project,
        scale_second,
    ) = [columns[i] for i in range(10)]
    bias_hidden = columns[10 : 10 + parts].reshape(parts, 1, width)
    weight_qkv = lax.dynamic_slice_in_dim(attention_full, core * 3 * half, 3 * half, 1)
    weight_output = attention_full[:, 3 * width : 4 * width]

    normed_window = layer_norm(window_tokens.astype(f32), gain_first, bias_first).astype(bf16)
    start = core * half
    bias_qkv = jnp.concatenate(
        [
            lax.dynamic_slice_in_dim(bias_query, start, half),
            jnp.zeros((half,), f32),
            lax.dynamic_slice_in_dim(bias_value, start, half),
        ]
    )
    scale_qkv = jnp.concatenate([jnp.full((half,), HEAD_DIM**-0.5, f32), jnp.ones((2 * half,), f32)])
    projected = ((product(normed_window, weight_qkv) + bias_qkv) * scale_qkv).astype(bf16)

    pairs = half // PAIR
    first = first_row // BLK

    def own_rows(group, lanes=half):
        return pl.BlockSpec((BLK, lanes), lambda h, b, lo, hi: (first + b, group * (half // lanes) + h))

    def all_rows(group, lanes=half):
        return pl.BlockSpec((window, lanes), lambda h, b, lo, hi: (0, group * (half // lanes) + h))

    row_block = pl.BlockSpec((BLK, half), lambda h, b, lo, hi: (b, 0))
    label_rows = pl.BlockSpec((BLK, 1), lambda h, b, lo, hi: (first + b, 0))
    label_all = pl.BlockSpec((1, window), lambda h, b, lo, hi: (0, 0))
    lanes = half // 2
    heads = lanes // HEAD_DIM
    half_block = pl.BlockSpec((BLK, lanes), lambda h, b, lo, hi: (b, h))
    attended_f, lse = attention_call(
        partial(attend_kernel, first),
        (half // lanes, own_blocks),
        [own_rows(0, lanes), all_rows(1, lanes), all_rows(2, lanes), label_rows, label_all],
        [half_block, half_block],
        [jax.ShapeDtypeStruct((2 * rows, half), f32)] * 2,
        [pltpu.VMEM((heads, window // STEP, BLK, STEP), f32)] + [pltpu.VMEM((heads, BLK, PAIR), f32)] * 3,
        50_000_000_000,
    )(lo, hi, projected, projected, projected, query_label[:, None], key_label[None])

    def columns_of(c, mine, theirs):
        return jnp.where(c == 0, jnp.concatenate([mine, theirs], 1), jnp.concatenate([theirs, mine], 1))

    attended_half = attended_f.astype(bf16)
    one_column = (jnp.arange(2 * pairs)[:, None] * HEAD_DIM == jnp.arange(half)[None]).astype(f32)
    lse_rows = lax.dot_general(one_column, lse, (((1,), (1,)), ((), ())), precision=lax.Precision.HIGHEST)
    attended_low = columns_of(
        core,
        lax.dynamic_slice_in_dim(attended_half, core * rows, rows, 0),
        swap(lax.dynamic_slice_in_dim(attended_half, (1 - core) * rows, rows, 0), 0),
    )
    inputs = tokens.astype(f32)
    branch = product(attended_low, weight_output) + bias_output
    middle = inputs + scale_first * branch

    normed_two, second_norm_back = jax.vjp(layer_norm, middle, gain_second, bias_second)
    upstream = cotangent.astype(f32)
    grad_dense = (upstream * scale_second).astype(bf16)
    chip_tokens = window_tokens[first_row:last_row].astype(f32)
    chip_center = chip_tokens - jnp.mean(chip_tokens, axis=-1, keepdims=True)
    chip_inverse = lax.rsqrt(jnp.mean(chip_center * chip_center, axis=-1, keepdims=True) + norm_eps)
    chip_unit = chip_center * chip_inverse
    normed_two_low, lse_rows, chip_unit, chip_inverse = lax.optimization_barrier(
        (normed_two.astype(bf16), lse_rows, chip_unit, chip_inverse)
    )
    active, grad_normed_two, dense_weight_grads, hidden_bias_grad = dense_call(
        normed_two_low, grad_dense, dense_full, bias_hidden
    )
    project_bias_grad = column_sums(grad_dense)
    grad_middle_norm, second_gain_grad, second_bias_grad = second_norm_back(grad_normed_two)
    grad_middle = upstream + grad_middle_norm
    grad_branch = (grad_middle * scale_first).astype(bf16)
    grad_attended = against(grad_branch, weight_output).astype(bf16)

    dense_sums = lax.psum_scatter(dense_weight_grads, "dev", scatter_dimension=1, tiled=True)
    bits = list(range(depth - 1, -1, -1))
    chips = bits[:-1][::-1]
    axes, far_bits = chips[:3], chips[3:]

    output_weight_grad = inner_rows(attended_low, grad_branch).astype(bf16)
    output_kept, output_other = halves([output_weight_grad.reshape((2,) * depth + (shard, width))], bits, 0)

    grad_half = jnp.where(core == 0, grad_attended[:, :half], grad_attended[:, half:])
    grad_other = swap(jnp.where(core == 0, grad_attended[:, half:], grad_attended[:, :half]), 0)
    grad_pair = jnp.where(
        core == 0, jnp.concatenate([grad_half, grad_other]), jnp.concatenate([grad_other, grad_half])
    )
    member = (jnp.arange(2 * pairs)[:, None] == jnp.arange(half)[None] // HEAD_DIM).astype(f32)
    delta = lax.dot_general(
        member, grad_pair.astype(f32) * attended_f, (((1,), (1,)), ((), ())), precision=lax.Precision.HIGHEST
    )
    stats = jnp.stack([lse_rows.reshape(pairs, 2, -1), delta.reshape(pairs, 2, -1)], axis=1).reshape(4 * pairs, -1)
    top = lax.reduce_precision(stats, 8, 7)
    mid = lax.reduce_precision(stats - top, 8, 7)
    pieces = jnp.concatenate([top, mid, stats - top - mid]).astype(bf16)
    stat_count = pieces.shape[0]
    packed = [jnp.concatenate([grad_pair[c * rows : (c + 1) * rows], pieces[:, c * rows : (c + 1) * rows]]) for c in range(2)]
    both = jnp.concatenate(packed)
    from_below = shifted(both, 2)
    from_above = shifted(both, -2)
    far_below = shifted(packed[1][rows - far_rows :], 4)
    far_above = shifted(jnp.concatenate([packed[0][:far_rows], packed[0][rows:]]), -4)
    (grad_queries,) = attention_call(
        partial(query_kernel, first),
        (1, own_blocks),
        [own_rows(0), all_rows(1), all_rows(2), label_rows, label_all, row_block, row_block, row_block],
        [row_block],
        [jax.ShapeDtypeStruct((2 * rows, half), bf16)],
        [pltpu.VMEM((2 * pairs, BLK, PAIR), f32)],
        60_000_000_000,
    )(lo, hi, projected, projected, projected, query_label[:, None], key_label[None], grad_pair, lse, attended_f)
    from_below, from_above, far_below, far_above, output_other, grad_queries = lax.optimization_barrier(
        (from_below, from_above, far_below, far_above, output_other, grad_queries)
    )
    normed_pair = normed_window[first_row:last_row]
    chip_view = (2,) * (depth - 1) + (2 * shard, half)

    def weight_sum(grad):
        return inner_rows(normed_pair, grad).astype(bf16).reshape(chip_view)

    output_chip = added(output_kept, output_other)
    output_chip = jnp.concatenate([output_chip[..., :half], output_chip[..., half:]], axis=-2)
    first_part = Travelling(
        jnp.concatenate([weight_sum(grad_queries), output_chip], axis=-1),
        bits[:-1],
        [axes[2]] + far_bits + [axes[0], axes[1]],
    )
    first_part.send()
    unit = rows + stat_count
    own_unit = both
    stat_parts = [far_below[far_rows:]]
    for piece in (from_below, own_unit, from_above):
        stat_parts += [piece[rows:unit], piece[unit + rows :]]
    stat_parts.append(far_above[far_rows:])
    stat_window = jnp.concatenate(stat_parts, axis=1).astype(f32)
    third = 4 * pairs
    stat_window = stat_window[:third] + stat_window[third : 2 * third] + stat_window[2 * third :]
    one_unit = pl.BlockSpec((far_rows + stat_count, half), lambda h, b, lo, hi: (0, 0))
    two_units = pl.BlockSpec((2 * unit, half), lambda h, b, lo, hi: (0, 0))
    grad_keys, grad_values = attention_call(
        partial(key_kernel, first, stat_count),
        (1, own_blocks),
        [
            all_rows(0),
            own_rows(1),
            own_rows(2),
            label_all,
            label_rows,
            one_unit,
            two_units,
            two_units,
            two_units,
            one_unit,
            pl.BlockSpec((4 * pairs, window), lambda h, b, lo, hi: (0, 0)),
        ],
        [row_block, row_block],
        [jax.ShapeDtypeStruct((2 * rows, half), bf16)] * 2,
        [pltpu.VMEM((2 * pairs, BLK, PAIR), f32)] * 2 + [pltpu.VMEM((window, half), bf16)],
        70_000_000_000,
    )(lo, hi, projected, projected, projected, query_label[None], key_label[:, None], far_below, from_below, own_unit, from_above, far_above, stat_window)

    grad_keys, grad_values, grad_branch, grad_middle, active = first_part.receive(
        grad_keys, grad_values, grad_branch, grad_middle, active
    )
    key_part = Travelling(weight_sum(grad_keys), bits[:-1], [axes[0], axes[1], axes[2]] + far_bits)
    value_part = Travelling(weight_sum(grad_values), bits[:-1], [axes[1], axes[2], axes[0]] + far_bits)
    for part in (key_part, value_part, first_part):
        part.send()
    grad_all = jnp.concatenate([grad_queries, grad_keys, grad_values], axis=1)
    grad_normed_pair = against(grad_all, weight_qkv)
    grad_normed_own = lax.dynamic_slice_in_dim(grad_normed_pair, core * rows, rows, 0)
    grad_normed_other = swap(lax.dynamic_slice_in_dim(grad_normed_pair, (1 - core) * rows, rows, 0), 0)
    first_gain_grad = jnp.sum(grad_normed_pair * chip_unit, axis=0)
    first_bias_grad = jnp.sum(grad_normed_pair, axis=0)
    output_bias_grad = column_sums(grad_branch)
    attention_scale_grad = jnp.sum(grad_middle * branch, axis=0)
    dense_out = sum_call(forward_sum_kernel, active, dense_full, parts) + bias_project
    layer_output = (middle + scale_second * dense_out).astype(bf16)
    dense_scale_grad = jnp.sum(upstream * dense_out, axis=0)

    def placed_half(values):
        spread = jnp.zeros((width,), f32)
        return lax.dynamic_update_slice_in_dim(spread, values, core * half, 0)

    grads = [
        first_gain_grad,
        first_bias_grad,
        placed_half(column_sums(grad_queries)),
        placed_half(column_sums(grad_values)),
        output_bias_grad,
        attention_scale_grad,
        second_gain_grad,
        second_bias_grad,
        project_bias_grad,
        dense_scale_grad,
        hidden_bias_grad.reshape(parts, count, shard).transpose(1, 0, 2),
    ]
    vector_rows = jnp.concatenate([g.reshape(count, -1) for g in grads], axis=1)
    vector_rows = jnp.pad(vector_rows, ((0, 0), (0, -vector_rows.shape[1] % 128)))
    vector_part = Travelling(vector_rows.reshape((2,) * depth + (1, -1)), bits, bits[::-1], f32)
    vector_part.send()
    grad_normed_own, grad_normed_other, layer_output = received(
        (key_part, value_part, first_part, vector_part), grad_normed_own, grad_normed_other, layer_output
    )
    for part in (key_part, value_part, first_part, vector_part):
        part.send()

    grad_normed = grad_normed_own + grad_normed_other
    unit_rows = lax.dynamic_slice_in_dim(chip_unit, core * rows, rows, 0)
    inverse = lax.dynamic_slice_in_dim(chip_inverse, core * rows, rows, 0)
    gained = grad_normed * gain_first
    along = jnp.mean(gained * unit_rows, axis=-1, keepdims=True)
    gained = gained - jnp.mean(gained, axis=-1, keepdims=True) - unit_rows * along
    input_gradient = grad_middle + gained * inverse

    moving = [key_part, value_part, first_part, vector_part]
    swapped = {}

    def to_core(name, part):
        kept = lax.dynamic_slice_in_dim(part.block, core * shard, shard, 0)
        sent = lax.dynamic_slice_in_dim(part.block, (1 - core) * shard, shard, 0)
        if name == "first":
            swapped["output"] = part.block[:, half:]
            kept, sent = kept[:, :half], sent[:, :half]
        swapped[name] = (kept, swap(sent, 0))

    names = {id(key_part): "key", id(value_part): "value", id(first_part): "first"}
    turn = 0
    while moving:
        if turn == 0:
            input_gradient, dense_sums = received(moving, input_gradient, dense_sums)
            project_out = dense_sums[parts:].reshape(parts * shard, width).astype(f32)
            if parts * shard == 128:
                hidden_out = pl.pallas_call(ungroup_kernel, out_shape=jax.ShapeDtypeStruct((shard, ff), f32))(
                    dense_sums[:parts]
                )
            else:
                hidden_out = dense_sums[:parts].reshape(parts, shard, count, shard)
                hidden_out = hidden_out.transpose(1, 2, 0, 3).reshape(shard, ff).astype(f32)
        elif turn == 1:
            project_out, hidden_out = received(moving, project_out, hidden_out)
        else:
            received(moving)
        still = []
        for part in moving:
            if part.order:
                part.send()
                still.append(part)
            elif id(part) in names:
                to_core(names[id(part)], part)
        moving = still
        turn += 1
    query_out, key_out, value_out = [columns_of(core, *swapped[n]).astype(f32) for n in ("first", "key", "value")]
    output_out = jnp.concatenate([swapped["output"][:shard], swapped["output"][shard:]], axis=1).astype(f32)
    vector_sum = vector_part.block[0]
    out = [vector_sum[i * shard : (i + 1) * shard] for i in range(10)]
    hidden_bias_out = vector_sum[10 * shard : (10 + parts) * shard]
    return (
        layer_output,
        input_gradient,
        out[0],
        out[1],
        query_out,
        out[2],
        key_out,
        value_out,
        out[3],
        output_out,
        out[4],
        out[5],
        out[6],
        out[7],
        hidden_out,
        hidden_bias_out,
        project_out,
        out[8],
        out[9],
    )


def solution(mesh):
    placed = (
        P("dev", None),
        P("dev", None),
        P("dev"),
        P("dev"),
        P("dev"),
        P("dev"),
        P("dev", None),
        P("dev"),
        P("dev", None),
        P("dev", None),
        P("dev"),
        P("dev", None),
        P("dev"),
        P("dev"),
        P("dev"),
        P("dev"),
        P("dev", None),
        P("dev"),
        P("dev", None),
        P("dev"),
        P("dev"),
    )
    return jax.shard_map(
        on_device,
        mesh=mesh,
        in_specs=placed,
        out_specs=(
            P("dev", None),
            P("dev", None),
            P("dev"),
            P("dev"),
            P("dev", None),
            P("dev"),
            P("dev", None),
            P("dev", None),
            P("dev"),
            P("dev", None),
            P("dev"),
            P("dev"),
            P("dev"),
            P("dev"),
            P("dev", None),
            P("dev"),
            P("dev", None),
            P("dev"),
            P("dev"),
        ),
        check_vma=False,
    )
```
